128 devices in a mesh: rep: 16 (over z, x), tp: 8 (over y, core).
Axes of the slice: x: 4, y: 4, z: 4, core: 2. Of those that a mesh axis runs over, the one named last changes fastest.
Arguments:
- activations: bfloat16 [16384, 8192], P('rep'), may hold values from -6 to 6
- token_adapter_index: int32 [16384, 1], P('rep'), may hold values from 0 to 31; in each aligned block of 1024 rows (0 to 1023, 1024 to 2047, ...) at most 64 rows name the same one
- query_matrix: bfloat16 [8192, 4096], P(None, 'tp'), may hold values from -0.0625 to 0.0625
- adapter_down_factor: bfloat16 [32, 8192, 64], P('rep', 'tp'), may hold values from -0.0625 to 0.0625
- adapter_up_factor: bfloat16 [32, 64, 4096], P('rep', None, 'tp'), may hold values from -0.75 to 0.75
Outputs:
- queries: bfloat16 [16384, 4096], P('rep', 'tp')
The draws below stay inside these ranges and needn't reach their ends.
Inputs may be any that keep to these rules, and one draw needn't show every extreme that they name: `token_adapter_index`: in the rows of one replica (1024 tokens), no adapter appears more than 64 times, and one appears exactly 64 times; every adapter appears somewhere.
All inputs are finite; a program needn't handle non-finite values.
Results may differ from the reference program's by a relative error of at most 0.0036.
Values may be sent and summed in bfloat16 or wider, within the bound.
No kernel may reach another device: no remote copies, remote signals or barrier semaphores. Data moves between devices by JAX's collectives and lax.ppermute only.
A program may use at most 128 MiB of HBM per device.

```python
import math
import jax
import jax.numpy as jnp
import numpy as np
from jax import lax

MODEL_WIDTH = 8192
QUERY_COLUMNS = 4096
ADAPTER_RANK = 64
ROWS = 1024
ADAPTER_TOTAL = 32
MOST = 64
TOKENS = 16384
N_REP = 16


def block_scale(stream_key, dims, shards, least, largest):
    def one(axis_at, blocks):
        draws = jax.random.uniform(jax.random.fold_in(jax.random.fold_in(stream_key, 6), axis_at), (blocks,), jnp.float32, least / len(shards), largest / len(shards))
        return jnp.repeat(jnp.exp(draws), dims[axis_at] // blocks).reshape((-1,) + (1,) * (len(dims) - axis_at - 1))

    level = one(*shards[0])
    for cut in shards[1:]:
        level = level * one(*cut)
    return level


def routed_block(stream_key, own, number, rows, amount, top, bound, lean):
    ranking = jax.random.permutation(stream_key, amount)
    heavy_load, usual = portions_of(amount, rows * top, bound, lean, True), portions_of(amount, rows * top, bound, lean, False)
    places = jnp.arange(amount)

    def named(tallies, offset_by):
        used = int((tallies > 0).sum())
        fixed = max(1, used // 4)
        moved = fixed + (places - fixed + offset_by * (used - fixed)) % max(1, amount - fixed)
        return jnp.zeros((amount,), jnp.int32).at[ranking[jnp.where(places < fixed, places, moved)]].set(jnp.asarray(tallies, jnp.int32))

    tallies = jnp.where(number % 4 == 0, named(heavy_load, number // 4), named(usual, number - number // 4 - 1))
    mixed = jax.random.permutation(jax.random.fold_in(own, 3), amount)
    source_of, taker = mixed[0:amount // 2 * 2:2], mixed[1:amount // 2 * 2:2]
    margin = jnp.minimum(tallies[source_of] - 1, bound - tallies[taker]) // 2
    margin = jnp.where((source_of == ranking[0]) | (taker == ranking[0]) | (tallies[taker] == 0), 0, jnp.maximum(margin, 0))
    moved = jax.random.randint(jax.random.fold_in(own, 4), (amount // 2,), 0, 1 << 20) % (margin + 1)
    tallies = tallies.at[source_of].add(-moved).at[taker].add(moved)
    labels = jnp.searchsorted(jnp.cumsum(tallies), jnp.arange(rows * top), side="right").astype(jnp.int32)
    table = labels.reshape(top, rows).T
    table = table[jax.random.permutation(jax.random.fold_in(own, 1), rows)]
    offset_by = jax.random.randint(jax.random.fold_in(own, 2), (rows, 1), 0, top)
    return jnp.take_along_axis(table, (jnp.arange(top)[None, :] + offset_by) % top, axis=1)


def portions_of(count, total, reach, lean, full):
    portions = [(1 << 20) // math.isqrt(grade ** lean) + 1 for grade in range(1, count + 1)]
    largest = reach if full else min(reach, max(-(-total // count), total * portions[0] // sum(portions)))
    least = 1 if total - largest >= count - 1 else 0
    holding, rest = [largest] + [least] * (count - 1), total - largest - least * (count - 1)
    while rest > 0:
        movable = [i for i in range(1, count) if holding[i] < largest] or [i for i in range(1, count) if holding[i] < reach]
        pool, left = sum([portions[i] for i in movable]), rest
        for i in movable:
            addition = min(reach - holding[i], max(1, left * portions[i] // pool), rest)
            holding[i] = holding[i] + addition
            rest = rest - addition
    return np.array(holding)


def scatter_about(key, extent, spread, bound, split=(), held_as=jnp.bfloat16):
    factor_of = block_scale(key, extent, split, -0.22, 0.18) if split else 1.0
    entries = jax.random.normal(key, extent, jnp.float32) * spread * factor_of
    return jnp.minimum(jnp.maximum(entries, -bound), bound).astype(held_as)


def setup_inputs(seed: int = 0) -> dict:
    streams_of = jax.random.split(jax.random.key(seed), 6)
    activations = scatter_about(streams_of[0], (TOKENS, MODEL_WIDTH), 1.0, 6.0, ((0, 16),))
    token_adapter_index_keys = jax.random.split(jax.random.fold_in(streams_of[1], 1), TOKENS // ROWS)
    token_adapter_index_turns = jax.random.permutation(jax.random.fold_in(streams_of[1], 3), TOKENS // ROWS)
    token_adapter_index = jax.vmap(lambda own, number: routed_block(jax.random.fold_in(streams_of[1], 2), own, number, ROWS, ADAPTER_TOTAL, 1, MOST, 2))(token_adapter_index_keys, token_adapter_index_turns).reshape((TOKENS, 1))
    query_matrix = scatter_about(streams_of[2], (MODEL_WIDTH, QUERY_COLUMNS), MODEL_WIDTH ** -0.5, 0.0625, ((1, 8),))
    adapter_down_factor = scatter_about(streams_of[3], (ADAPTER_TOTAL, MODEL_WIDTH, ADAPTER_RANK), MODEL_WIDTH ** -0.5, 0.0625, ((0, 16), (1, 8)))
    adapter_up_factor = scatter_about(streams_of[4], (ADAPTER_TOTAL, ADAPTER_RANK, QUERY_COLUMNS), ADAPTER_RANK ** -0.5, 0.75, ((0, 16), (2, 8)))
    return {"activations": activations, "token_adapter_index": token_adapter_index, "query_matrix": query_matrix, "adapter_down_factor": adapter_down_factor, "adapter_up_factor": adapter_up_factor}


adapter_scale = 0.5


def reference(activations, token_adapter_index, query_matrix, adapter_down_factor, adapter_up_factor):
    ident = token_adapter_index[:, 0].astype(jnp.int32)
    tokens = ident.shape[0]
    adapter_table = adapter_down_factor.shape[0]
    capacity = N_REP * MOST
    onehot = (ident[:, None] == jnp.arange(adapter_table, dtype=jnp.int32)[None, :]).astype(jnp.int32)
    rank = jnp.sum((jnp.cumsum(onehot, axis=0) - onehot) * onehot, axis=1).astype(jnp.int32)
    slots = (ident * capacity + rank).astype(jnp.int32)
    token_of_slot = jnp.full((adapter_table * capacity,), tokens, jnp.int32)
    token_of_slot = token_of_slot.at[slots].set(jnp.arange(tokens, dtype=jnp.int32)).reshape(adapter_table, capacity)
    padded = jnp.concatenate([activations, jnp.zeros((1, activations.shape[1]), activations.dtype)], axis=0)

    def one_adapter(group_index):
        token_rows = padded[token_of_slot[group_index]]
        shrunk_rows = jnp.dot(token_rows, adapter_down_factor[group_index], preferred_element_type=jnp.float32).astype(jnp.bfloat16)
        return jnp.dot(shrunk_rows, adapter_up_factor[group_index], preferred_element_type=jnp.float32).astype(jnp.bfloat16)

    delta = lax.map(one_adapter, jnp.arange(adapter_table, dtype=jnp.int32))
    token_delta = delta.reshape(adapter_table * capacity, -1)[slots]
    base_output = jnp.dot(activations, query_matrix, preferred_element_type=jnp.float32)
    return (base_output + adapter_scale * token_delta.astype(jnp.float32)).astype(jnp.bfloat16)
```

```python
import functools

import jax
import jax.numpy as jnp
from jax import lax
from jax.experimental import pallas as pl
from jax.experimental.pallas import tpu as pltpu
from jax.sharding import PartitionSpec as P

BF, F32 = jnp.bfloat16, jnp.float32
AXES = ("rep", "tp")
RING = 4
adapter_scale = 0.5


def device_of(x, y, z, c):
    return (z % RING * RING + x % RING) * 2 * RING + y % RING * 2 + c


def every(f):
    return [
        (device_of(x, y, z, c), device_of(*f(x, y, z, c)))
        for z in range(RING)
        for x in range(RING)
        for y in range(RING)
        for c in range(2)
    ]


def first(a, d):
    return lax.ppermute(
        a, AXES, every(lambda x, y, z, c: (x, y, z + d, c) if c else (x + d, y, z, c))
    )


def second(a, d):
    return lax.ppermute(
        a, AXES, every(lambda x, y, z, c: (x + d, y, z, c) if c else (x, y, z + d, c))
    )


def other_core(a):
    return lax.ppermute(a, AXES, every(lambda x, y, z, c: (x, y, z, 1 - c)))


def pair(a, step):
    def to(x, y, z, c):
        return (x, (y ^ 1) if (c + step) % 2 == 0 else (3 - y), z, c)
    return lax.ppermute(a, AXES, every(to))


def params():
    return pltpu.CompilerParams(vmem_limit_bytes=48 << 20)


def base_kernel(x_ref, w_ref, o_ref):
    p = jnp.dot(x_ref[...], w_ref[...], preferred_element_type=F32)

    @pl.when(pl.program_id(0) == 0)
    def _():
        o_ref[...] = p

    @pl.when(pl.program_id(0) > 0)
    def _():
        o_ref[...] += p


def base_product(x, w, depth=2048):
    m, k = x.shape
    n = w.shape[1]
    return pl.pallas_call(
        base_kernel,
        grid=(k // depth,),
        in_specs=[
            pl.BlockSpec((m, depth), lambda i: (0, i)),
            pl.BlockSpec((depth, n), lambda i: (i, 0)),
        ],
        out_specs=pl.BlockSpec((m, n), lambda i: (0, 0)),
        out_shape=jax.ShapeDtypeStruct((m, n), F32),
        compiler_params=params(),
        cost_estimate=pl.CostEstimate(
            flops=2 * m * n * k, bytes_accessed=2 * (m * k + k * n) + 4 * m * n, transcendentals=0
        ),
        name="base",
    )(x, w)


def shrink_kernel(counts, has_sum, last, s_ref, code_ref, x_ref, *refs):
    a_refs, refs = refs[: len(counts)], refs[len(counts):]
    o_ref = refs[-1]
    code = code_ref[...]
    total = refs[0][...] if has_sum else None
    at = 0
    for a_ref, count in zip(a_refs, counts):
        p = lax.dot_general(
            x_ref[...], a_ref[...], (((1,), (1,)), ((), ())), preferred_element_type=F32
        )
        for j in range(count):
            term = jnp.where(code == s_ref[at + j], p[:, 128 * j : 128 * j + 128], 0.0)
            total = term if total is None else total + term
        at += count
    if last:
        half = total.shape[0] // 2
        folded = total + pltpu.roll(total, 64, 1)
        lane = lax.broadcasted_iota(jnp.int32, (half, 128), 1)
        o_ref[...] = jnp.where(lane < 64, folded[:half], folded[half:])
    else:
        o_ref[...] = total


def shrink(code, where, ids, x, parts, total, last, name):
    m, width = x.shape[0], parts[0].shape[1]
    width = min(width, 1024)
    counts = tuple(a.shape[0] // 128 for a in parts)
    nb = sum(counts)
    s = jnp.concatenate([ids, where[None]])
    whole = lambda i, s: (0, 0)
    specs = [pl.BlockSpec((m, 128), whole), pl.BlockSpec((m, width), lambda i, s: (0, s[nb]))]
    specs += [pl.BlockSpec((a.shape[0], width), whole) for a in parts]
    args = [s, code, x, *parts]
    if total is not None:
        specs.append(pl.BlockSpec((m, 128), whole))
        args.append(total)
    rows = m // 2 if last else m
    return pl.pallas_call(
        functools.partial(shrink_kernel, counts, total is not None, last),
        grid_spec=pltpu.PrefetchScalarGridSpec(
            num_scalar_prefetch=1,
            grid=(1,),
            in_specs=specs,
            out_specs=pl.BlockSpec((rows, 128), whole),
        ),
        out_shape=jax.ShapeDtypeStruct((rows, 128), F32),
        compiler_params=params(),
        cost_estimate=pl.CostEstimate(
            flops=2 * m * width * nb * 128, bytes_accessed=2 * m * width + 256 * nb * width, transcendentals=0
        ),
        name=name,
    )(*args)


def expand_kernel(counts, s_ref, code_ref, mine_ref, other_ref, base_ref, *refs):
    b_refs, o_ref = refs[:-1], refs[-1]
    code = code_ref[...]
    packed = mine_ref[...] + other_ref[...]
    lane = lax.broadcasted_iota(jnp.int32, packed.shape, 1)
    left = (lane < 64) == (pl.program_id(0) < pl.num_programs(0) // 2)
    rows = jnp.where(left, packed, pltpu.roll(packed, 64, 1))
    delta, at = None, 0
    for b_ref, count in zip(b_refs, counts):
        spread = jnp.concatenate(
            [jnp.where(code == s_ref[at + j], rows, 0.0).astype(BF) for j in range(count)], axis=1
        )
        d = jnp.dot(spread, b_ref[...], preferred_element_type=F32)
        delta = d if delta is None else delta + d
        at += count
    delta = delta.astype(BF).astype(F32)
    o_ref[...] = (base_ref[...] + adapter_scale * delta).astype(BF)


def expand(code, ids, mine, other, base, parts, block=256):
    m, n = base.shape
    counts = tuple(b.shape[0] // 128 for b in parts)
    steps = m // block
    row = lambda i, s: (i, 0)
    packed = pl.BlockSpec((block, 128), lambda i, s: (i % (steps // 2), 0))
    specs = [pl.BlockSpec((block, 128), row), packed, packed, pl.BlockSpec((block, n), row)]
    specs += [pl.BlockSpec((b.shape[0], n), lambda i, s: (0, 0)) for b in parts]
    return pl.pallas_call(
        functools.partial(expand_kernel, counts),
        grid_spec=pltpu.PrefetchScalarGridSpec(
            num_scalar_prefetch=1,
            grid=(steps,),
            in_specs=specs,
            out_specs=pl.BlockSpec((block, n), row),
        ),
        out_shape=jax.ShapeDtypeStruct((m, n), BF),
        compiler_params=params(),
        cost_estimate=pl.CostEstimate(
            flops=2 * m * n * 128 * sum(counts), bytes_accessed=6 * m * n, transcendentals=0
        ),
        name="expand",
    )(ids, code, mine, other, base, *parts)


def per_device(activations, token_adapter_index, query_matrix, down, up):
    m = activations.shape[0]
    rep, tp = lax.axis_index("rep"), lax.axis_index("tp")
    core = tp % 2
    hops = jnp.array([0, -1, 1, 2], jnp.int32)
    z, x = rep // RING, rep % RING
    zs, xs = (z + hops) % RING, (x + hops) % RING
    ids = jnp.where(core == 0, zs[:, None] * RING + xs[None, :], zs[None, :] * RING + xs[:, None])
    ids = ids.reshape(16)
    ident = token_adapter_index
    side = lax.broadcasted_iota(jnp.int32, (m, 128), 1) // 64
    code = jnp.where(ident % 2 == side, ident // 2, -1)

    down = jnp.swapaxes(down, 1, 2).reshape(128, -1)
    up = up.reshape(128, -1)

    def gather_first(a):
        return jnp.concatenate([a, first(a, 1), first(a, -1), first(a, 2)], axis=0)

    def gather_second(a):
        half = a.shape[0] // 2
        before, after = second(a, 1), second(a, -1)
        far = (second(before[:half], 1), second(after[half:], -1))
        return before, after, far

    both = gather_first(jnp.concatenate([down, up], axis=1))
    width = down.shape[1]
    d0, u0 = both[:, :width], both[:, width:]
    d1, d2, d3 = gather_second(d0)
    u1, u2, u3 = gather_second(u0)
    base = base_product(activations, query_matrix)
    total = shrink(code, tp, ids[:12], activations, [d0, d1, d2], None, False, "shrink_near")
    total = shrink(code, tp, ids[12:], activations, d3, total, True, "shrink_far")
    total = total + other_core(total)
    total = total + pair(total, 0)
    other = pair(total, 1)
    return expand(code, ids, total, other, base, [u0, u1, u2, *u3])


def solution(mesh):
    in_specs = (
        P("rep", None),
        P("rep", None),
        P(None, "tp"),
        P("rep", "tp", None),
        P("rep", None, "tp"),
    )
    return jax.shard_map(
        per_device, mesh=mesh, in_specs=in_specs, out_specs=P("rep", "tp"), check_vma=False
    )
```

```python
import functools

import jax
import jax.numpy as jnp
from jax import lax
from jax.experimental import pallas as pl
from jax.experimental.pallas import tpu as pltpu
from jax.sharding import PartitionSpec as P

BF, F32 = jnp.bfloat16, jnp.float32
AXES = ("rep", "tp")
RING = 4
adapter_scale = 0.5


def device_of(x, y, z, c):
    return (z % RING * RING + x % RING) * 2 * RING + y % RING * 2 + c


def every(f):
    return [
        (device_of(x, y, z, c), device_of(*f(x, y, z, c)))
        for z in range(RING)
        for x in range(RING)
        for y in range(RING)
        for c in range(2)
    ]


def first(a, d):
    return lax.ppermute(
        a, AXES, every(lambda x, y, z, c: (x, y, z + d, c) if c else (x + d, y, z, c))
    )


def second(a, d):
    return lax.ppermute(
        a, AXES, every(lambda x, y, z, c: (x + d, y, z, c) if c else (x, y, z + d, c))
    )


def other_core(a):
    return lax.ppermute(a, AXES, every(lambda x, y, z, c: (x, y, z, 1 - c)))


def pair(a, step):
    def to(x, y, z, c):
        return (x, (y ^ 1) if (c + step) % 2 == 0 else (3 - y), z, c)
    return lax.ppermute(a, AXES, every(to))


def params():
    return pltpu.CompilerParams(vmem_limit_bytes=48 << 20)


def base_kernel(x_ref, w_ref, o_ref):
    p = jnp.dot(x_ref[...], w_ref[...], preferred_element_type=F32)

    @pl.when(pl.program_id(0) == 0)
    def _():
        o_ref[...] = p

    @pl.when(pl.program_id(0) > 0)
    def _():
        o_ref[...] += p


def base_product(x, w, depth=2048):
    m, k = x.shape
    n = w.shape[1]
    return pl.pallas_call(
        base_kernel,
        grid=(k // depth,),
        in_specs=[
            pl.BlockSpec((m, depth), lambda i: (0, i)),
            pl.BlockSpec((depth, n), lambda i: (i, 0)),
        ],
        out_specs=pl.BlockSpec((m, n), lambda i: (0, 0)),
        out_shape=jax.ShapeDtypeStruct((m, n), F32),
        compiler_params=params(),
        cost_estimate=pl.CostEstimate(
            flops=2 * m * n * k, bytes_accessed=2 * (m * k + k * n) + 4 * m * n, transcendentals=0
        ),
        name="base",
    )(x, w)


def shrink_kernel(counts, has_sum, last, s_ref, code_ref, x_ref, *refs):
    a_refs, refs = refs[: len(counts)], refs[len(counts):]
    o_ref = refs[-1]
    code = code_ref[...]
    total = refs[0][...] if has_sum else None
    at = 0
    for a_ref, count in zip(a_refs, counts):
        p = lax.dot_general(
            x_ref[...], a_ref[...], (((1,), (1,)), ((), ())), preferred_element_type=F32
        )
        for j in range(count):
            term = jnp.where(code == s_ref[at + j], p[:, 128 * j : 128 * j + 128], 0.0)
            total = term if total is None else total + term
        at += count
    if last:
        half = total.shape[0] // 2
        folded = total + pltpu.roll(total, 64, 1)
        lane = lax.broadcasted_iota(jnp.int32, (half, 128), 1)
        o_ref[...] = jnp.where(lane < 64, folded[:half], folded[half:])
    else:
        o_ref[...] = total


def shrink(code, ids, x, parts, total, last, name):
    m, width = x.shape
    counts = tuple(a.shape[0] // 128 for a in parts)
    nb = sum(counts)
    args = [ids, code, x, *parts] + ([] if total is None else [total])
    vmem = pl.BlockSpec(memory_space=pltpu.VMEM)
    return pl.pallas_call(
        functools.partial(shrink_kernel, counts, total is not None, last),
        in_specs=[pl.BlockSpec(memory_space=pltpu.SMEM)] + [vmem] * (len(args) - 1),
        out_specs=vmem,
        out_shape=jax.ShapeDtypeStruct((m // 2 if last else m, 128), F32),
        compiler_params=params(),
        cost_estimate=pl.CostEstimate(
            flops=2 * m * width * nb * 128, bytes_accessed=2 * m * width + 256 * nb * width, transcendentals=0
        ),
        name=name,
    )(*args)


def expand_kernel(counts, s_ref, code_ref, mine_ref, other_ref, base_ref, *refs):
    b_refs, o_ref = refs[:-1], refs[-1]
    code = code_ref[...]
    packed = mine_ref[...] + other_ref[...]
    lane = lax.broadcasted_iota(jnp.int32, packed.shape, 1)
    left = (lane < 64) == (pl.program_id(0) < pl.num_programs(0) // 2)
    rows = jnp.where(left, packed, pltpu.roll(packed, 64, 1))
    delta, at = None, 0
    for b_ref, count in zip(b_refs, counts):
        spread = jnp.concatenate(
            [jnp.where(code == s_ref[at + j], rows, 0.0).astype(BF) for j in range(count)], axis=1
        )
        d = jnp.dot(spread, b_ref[...], preferred_element_type=F32)
        delta = d if delta is None else delta + d
        at += count
    delta = delta.astype(BF).astype(F32)
    o_ref[...] = (base_ref[...] + adapter_scale * delta).astype(BF)


def expand(code, ids, mine, other, base, parts, block=256):
    m, n = base.shape
    counts = tuple(b.shape[0] // 128 for b in parts)
    steps = m // block
    row = lambda i, s: (i, 0)
    packed = pl.BlockSpec((block, 128), lambda i, s: (i % (steps // 2), 0))
    specs = [pl.BlockSpec((block, 128), row), packed, packed, pl.BlockSpec((block, n), row)]
    specs += [pl.BlockSpec((b.shape[0], n), lambda i, s: (0, 0)) for b in parts]
    return pl.pallas_call(
        functools.partial(expand_kernel, counts),
        grid_spec=pltpu.PrefetchScalarGridSpec(
            num_scalar_prefetch=1,
            grid=(steps,),
            in_specs=specs,
            out_specs=pl.BlockSpec((block, n), row),
        ),
        out_shape=jax.ShapeDtypeStruct((m, n), BF),
        compiler_params=params(),
        cost_estimate=pl.CostEstimate(
            flops=2 * m * n * 128 * sum(counts), bytes_accessed=6 * m * n, transcendentals=0
        ),
        name="expand",
    )(ids, code, mine, other, base, *parts)


def per_device(activations, token_adapter_index, query_matrix, down, up):
    m = activations.shape[0]
    rep, tp = lax.axis_index("rep"), lax.axis_index("tp")
    core = tp % 2
    hops = jnp.array([0, -1, 1, 2], jnp.int32)
    z, x = rep // RING, rep % RING
    zs, xs = (z + hops) % RING, (x + hops) % RING
    ids = jnp.where(core == 0, zs[:, None] * RING + xs[None, :], zs[None, :] * RING + xs[:, None])
    ids = ids.reshape(16)
    ident = token_adapter_index
    side = lax.broadcasted_iota(jnp.int32, (m, 128), 1) // 64
    code = jnp.where(ident % 2 == side, ident // 2, -1)

    down = jnp.swapaxes(down, 1, 2).reshape(128, -1)
    up = up.reshape(128, -1)

    def gather_first(a):
        return jnp.concatenate([a, first(a, 1), first(a, -1), first(a, 2)], axis=0)

    def gather_second(a):
        return second(a, 1), second(a, -1)

    def forward(before, after):
        half = before.shape[0] // 2
        return second(before[:half], 1), second(after[half:], -1)

    width = down.shape[1]
    here = lax.dynamic_slice_in_dim(activations, tp * width, width, 1)
    d0 = gather_first(down)
    u0 = gather_first(up)
    d0, here, code = lax.optimization_barrier((d0, here, code))
    d1, d2 = gather_second(d0)
    base = base_product(activations, query_matrix)
    d1, d2, base = lax.optimization_barrier((d1, d2, base))
    d3 = forward(d1, d2)
    u1, u2 = gather_second(u0)
    total = shrink(code, ids[:12], here, [d0, d1, d2], None, False, "shrink_near")
    total = shrink(code, ids[12:], here, d3, total, True, "shrink_far")
    u3 = forward(u1, u2)
    total = total + other_core(total)
    total = total + pair(total, 0)
    other = pair(total, 1)
    return expand(code, ids, total, other, base, [u0, u1, u2, *u3])


def solution(mesh):
    in_specs = (
        P("rep", None),
        P("rep", None),
        P(None, "tp"),
        P("rep", "tp", None),
        P("rep", None, "tp"),
    )
    return jax.shard_map(
        per_device, mesh=mesh, in_specs=in_specs, out_specs=P("rep", "tp"), check_vma=False
    )
```

```python
import functools

import jax
import jax.numpy as jnp
from jax import lax
from jax.experimental import pallas as pl
from jax.experimental.pallas import tpu as pltpu
from jax.sharding import PartitionSpec as P

BF, F32 = jnp.bfloat16, jnp.float32
AXES = ("rep", "tp")
RING = 4
HOPS = (0, -1, 1, 2)
adapter_scale = 0.5


def device_of(x, y, z, c):
    return (z % RING * RING + x % RING) * 2 * RING + y % RING * 2 + c


def every(f):
    return [
        (device_of(x, y, z, c), device_of(*f(x, y, z, c)))
        for z in range(RING)
        for x in range(RING)
        for y in range(RING)
        for c in range(2)
    ]


def first(a, d):
    return lax.ppermute(
        a, AXES, every(lambda x, y, z, c: (x, y, z + d, c) if c else (x + d, y, z, c))
    )


def second(a, d):
    return lax.ppermute(
        a, AXES, every(lambda x, y, z, c: (x + d, y, z, c) if c else (x, y, z + d, c))
    )


def other_core(a):
    return lax.ppermute(a, AXES, every(lambda x, y, z, c: (x, y, z, 1 - c)))


def pair(a, step):
    def to(x, y, z, c):
        return (x, (y ^ 1) if (c + step) % 2 == 0 else (3 - y), z, c)

    return lax.ppermute(a, AXES, every(to))


def params(mib):
    return pltpu.CompilerParams(vmem_limit_bytes=mib << 20)


def cost(flops, moved):
    return pl.CostEstimate(flops=flops, bytes_accessed=moved, transcendentals=0)


VMEM = pl.BlockSpec(memory_space=pltpu.VMEM)
HBM = pl.BlockSpec(memory_space=pltpu.HBM)


def owner(j, i):
    rep, core = lax.axis_index("rep"), lax.axis_index("tp") % 2
    dz, dx = jnp.where(core == 0, j, i), jnp.where(core == 0, i, j)
    return (rep // RING + dz + RING) % RING * RING + (rep % RING + dx + RING) % RING


def prep_kernel(ident_ref, x_ref, here_ref, code_ref, sem):
    width = here_ref.shape[1]
    at = pl.multiple_of(lax.axis_index("tp") * width, width)
    copy = pltpu.make_async_copy(x_ref.at[:, pl.ds(at, width)], here_ref, sem)
    copy.start()
    side = lax.broadcasted_iota(jnp.int32, (128, 128), 1) // 64
    for r in range(ident_ref.shape[0]):
        ident = jnp.broadcast_to(ident_ref[r : r + 1, :], (128, 128)).T
        code_ref[128 * r : 128 * r + 128, :] = jnp.where((ident & 1) == side, ident >> 1, -1)
    copy.wait()


def prepare(ident, x, width):
    m = x.shape[0]
    return pl.pallas_call(
        prep_kernel,
        in_specs=[VMEM, HBM],
        out_specs=[VMEM, VMEM],
        out_shape=[
            jax.ShapeDtypeStruct((m, width), BF),
            jax.ShapeDtypeStruct((m, 128), jnp.int32),
        ],
        scratch_shapes=[pltpu.SemaphoreType.DMA],
        compiler_params=params(50),
        cost_estimate=cost(0, 4 * m * width),
        name="prepare",
    )(ident.reshape(m // 128, 128), x)


def base_kernel(depths, block, x_ref, w_ref, o_ref, xb, wb, sems):
    copies, at = [], 0
    for i, depth in enumerate(depths):
        part = pl.ds(at, depth)
        copies.append(
            (
                part,
                pltpu.make_async_copy(w_ref.at[part], wb.at[part], sems.at[2 * i]),
                pltpu.make_async_copy(x_ref.at[:, part], xb.at[:, part], sems.at[2 * i + 1]),
            )
        )
        at += depth
    for _, *pair_of in copies:
        for copy in pair_of:
            copy.start()
    for i, (part, *pair_of) in enumerate(copies):
        for copy in pair_of:
            copy.wait()

        def rows(r, _):
            row = pl.ds(pl.multiple_of(r * block, block), block)
            p = jnp.dot(xb[row, part], wb[part, :], preferred_element_type=F32)
            o_ref[row, :] = p if i == 0 else o_ref[row, :] + p
            return 0

        lax.fori_loop(0, x_ref.shape[0] // block, rows, 0)


def base_product(x, w, depths=(1024, 2048, 2048, 2048, 1024), block=256):
    m, k = x.shape
    n = w.shape[1]
    return pl.pallas_call(
        functools.partial(base_kernel, depths, block),
        in_specs=[HBM, HBM],
        out_specs=VMEM,
        out_shape=jax.ShapeDtypeStruct((m, n), F32),
        scratch_shapes=[
            pltpu.VMEM((m, k), BF),
            pltpu.VMEM((k, n), BF),
            pltpu.SemaphoreType.DMA((2 * len(depths),)),
        ],
        compiler_params=params(30),
        cost_estimate=cost(2 * m * n * k, 2 * (m * k + k * n) + 4 * m * n),
        name="base",
    )(x, w)


def shrink_kernel(groups, has_sum, last, code_ref, x_ref, *refs):
    code = code_ref[...]
    refs = list(refs)
    total = None
    for j, sizes in groups:
        parts = [refs.pop(0)[...] for _ in sizes]
        a = parts[0] if len(parts) == 1 else jnp.concatenate(parts, axis=0)
        p = lax.dot_general(x_ref[...], a, (((1,), (1,)), ((), ())), preferred_element_type=F32)
        for k, i in enumerate(HOPS):
            term = jnp.where(code == owner(j, i), p[:, 128 * k : 128 * k + 128], 0.0)
            total = term if total is None else total + term
    if has_sum:
        total = total + refs.pop(0)[...]
    if not last:
        refs[0][...] = total
        return
    keep_ref, give_ref = refs
    half = total.shape[0] // 2
    folded = total + pltpu.roll(total, 64, 1)
    lane = lax.broadcasted_iota(jnp.int32, (half, 128), 1)
    packed = jnp.where(lane < 64, folded[:half], folded[half:])
    low, high = packed[: half // 2], packed[half // 2 :]
    core = lax.axis_index("tp") % 2
    keep_ref[...] = jnp.where(core == 0, low, high)
    give_ref[...] = jnp.where(core == 0, high, low)


def shrink(code, x, groups, total, last, name):
    m, width = x.shape
    args = [code, x] + [a for _, parts in groups for a in parts] + ([] if total is None else [total])
    rows = m // 4 if last else m
    shape = jax.ShapeDtypeStruct((rows, 128), F32)
    return pl.pallas_call(
        functools.partial(
            shrink_kernel, [(j, [a.shape[0] for a in p]) for j, p in groups], total is not None, last
        ),
        in_specs=[VMEM] * len(args),
        out_specs=[VMEM] * 2 if last else VMEM,
        out_shape=[shape] * 2 if last else shape,
        compiler_params=params(16),
        cost_estimate=cost(2 * m * width * 512 * len(groups), 2 * m * width),
        name=name,
    )(*args)


def expand_kernel(code_ref, mine_ref, other_ref, base_ref, *refs):
    b_refs, o_ref = refs[:-1], refs[-1]
    block = o_ref.shape[0]
    step = pl.program_id(0)
    at = pl.multiple_of(step * block, block)
    code = code_ref[pl.ds(at, block), :]
    mine = step % 2 == lax.axis_index("tp") % 2
    packed = jnp.where(mine, mine_ref[...].astype(F32), other_ref[...].astype(F32))
    lane = lax.broadcasted_iota(jnp.int32, packed.shape, 1)
    left = (lane < 64) == (step < 2)
    rows = jnp.where(left, packed, pltpu.roll(packed, 64, 1))
    delta = None
    for j, b_ref in zip(HOPS, b_refs):
        spread = jnp.concatenate(
            [jnp.where(code == owner(j, i), rows, 0.0).astype(BF) for i in HOPS], axis=1
        )
        d = jnp.dot(spread, b_ref[...], preferred_element_type=F32)
        delta = d if delta is None else delta + d
    delta = delta.astype(BF).astype(F32)
    o_ref[...] = (base_ref[pl.ds(at, block), :] + adapter_scale * delta).astype(BF)


def expand(code, mine, other, base, parts):
    m, n = base.shape
    block = m // 4
    args = [code, mine, other, base, *parts]
    return pl.pallas_call(
        expand_kernel,
        grid=(4,),
        in_specs=[VMEM] * len(args),
        out_specs=pl.BlockSpec((block, n), lambda i: (i, 0)),
        out_shape=jax.ShapeDtypeStruct((m, n), BF),
        compiler_params=params(16),
        cost_estimate=cost(2 * m * n * 2048, 6 * m * n),
        name="expand",
    )(*args)


def after(a, *others):
    return lax.optimization_barrier((a, others))[0]


def per_device(activations, token_adapter_index, query_matrix, down, up):
    down = jnp.swapaxes(down, 1, 2).reshape(128, -1)
    up = up.reshape(128, -1)

    near = [first(down, d) for d in (1, -1, 2)]
    own = [second(down, d) for d in (1, -1)]
    up_near = [first(up, d) for d in (1, -1, 2)]
    here, code = prepare(token_adapter_index, activations, down.shape[1])
    near, up_near, here, code = lax.optimization_barrier((near, up_near, here, code))
    rest = jnp.concatenate(near, axis=0)
    d0 = jnp.concatenate([down, *near], axis=0)
    sides = [second(rest, d) for d in (1, -1)]
    far = second(d0, 2)

    base = base_product(activations, query_matrix)
    total = shrink(code, here, [(0, [d0])], None, False, "shrink_own")
    u0 = after(jnp.concatenate([up, *up_near], axis=0), base)
    ups = [u0] + [second(u0, d) for d in (1, -1, 2)]

    sides, total, base = lax.optimization_barrier((sides, total, base))
    total = shrink(
        code, here, [(-1, [own[0], sides[0]]), (1, [own[1], sides[1]])], total, False, "shrink_near"
    )
    far, total = lax.optimization_barrier((far, total))
    keep, give = shrink(code, here, [(2, [far])], total, True, "shrink_far")
    keep = keep + other_core(give)
    keep = keep + pair(keep, 0)
    keep = keep + pair(keep, 1)
    mine, ups = lax.optimization_barrier((keep.astype(BF), ups))
    return expand(code, mine, other_core(mine), base, ups)


def solution(mesh):
    in_specs = (
        P("rep", None),
        P("rep", None),
        P(None, "tp"),
        P("rep", "tp", None),
        P("rep", None, "tp"),
    )
    return jax.shard_map(
        per_device, mesh=mesh, in_specs=in_specs, out_specs=P("rep", "tp"), check_vma=False
    )
```

```python
import functools

import jax
import jax.numpy as jnp
from jax import lax
from jax.experimental import pallas as pl
from jax.experimental.pallas import tpu as pltpu
from jax.sharding import PartitionSpec as P

BF, F32 = jnp.bfloat16, jnp.float32
AXES = ("rep", "tp")
RING = 4
HOPS = (0, -1, 1, 2)
adapter_scale = 0.5


def device_of(x, y, z, c):
    return (z % RING * RING + x % RING) * 2 * RING + y % RING * 2 + c


def every(f):
    return [
        (device_of(x, y, z, c), device_of(*f(x, y, z, c)))
        for z in range(RING)
        for x in range(RING)
        for y in range(RING)
        for c in range(2)
    ]


def first(a, d):
    return lax.ppermute(
        a, AXES, every(lambda x, y, z, c: (x, y, z + d, c) if c else (x + d, y, z, c))
    )


def second(a, d):
    return lax.ppermute(
        a, AXES, every(lambda x, y, z, c: (x + d, y, z, c) if c else (x, y, z + d, c))
    )


def other_core(a):
    return lax.ppermute(a, AXES, every(lambda x, y, z, c: (x, y, z, 1 - c)))


def pair(a, step):
    def to(x, y, z, c):
        return (x, (y ^ 1) if (c + step) % 2 == 0 else (3 - y), z, c)

    return lax.ppermute(a, AXES, every(to))


def params(mib):
    return pltpu.CompilerParams(vmem_limit_bytes=mib << 20)


def cost(flops, moved):
    return pl.CostEstimate(flops=flops, bytes_accessed=moved, transcendentals=0)


VMEM = pl.BlockSpec(memory_space=pltpu.VMEM)
HBM = pl.BlockSpec(memory_space=pltpu.HBM)


def owner(j, i):
    rep, core = lax.axis_index("rep"), lax.axis_index("tp") % 2
    dz, dx = jnp.where(core == 0, j, i), jnp.where(core == 0, i, j)
    return (rep // RING + dz + RING) % RING * RING + (rep % RING + dx + RING) % RING


def prep_kernel(ident_ref, x_ref, here_ref, code_ref, sem):
    width = here_ref.shape[1]
    at = pl.multiple_of(lax.axis_index("tp") * width, width)
    copy = pltpu.make_async_copy(x_ref.at[:, pl.ds(at, width)], here_ref, sem)
    copy.start()
    side = lax.broadcasted_iota(jnp.int32, (128, 128), 1) // 64
    for r in range(ident_ref.shape[0]):
        ident = jnp.broadcast_to(ident_ref[r : r + 1, :], (128, 128)).T
        code_ref[128 * r : 128 * r + 128, :] = jnp.where((ident & 1) == side, ident >> 1, -1)
    copy.wait()


def prepare(ident, x, width):
    m = x.shape[0]
    return pl.pallas_call(
        prep_kernel,
        in_specs=[VMEM, HBM],
        out_specs=[VMEM, VMEM],
        out_shape=[
            jax.ShapeDtypeStruct((m, width), BF),
            jax.ShapeDtypeStruct((m, 128), jnp.int32),
        ],
        scratch_shapes=[pltpu.SemaphoreType.DMA],
        compiler_params=params(50),
        cost_estimate=cost(0, 1 << 20),
        name="prepare",
    )(ident.reshape(m // 128, 128), x)


def base_kernel(at, x_ref, w_ref, o_ref, xb, sems):
    count = sems.shape[0]
    block = xb.shape[0] // count
    copies = []
    for i in range(count):
        rows = pl.ds(i * block, block)
        copies.append(
            pltpu.make_async_copy(x_ref.at[pl.ds(at + i * block, block)], xb.at[rows], sems.at[i])
        )
    for copy in copies:
        copy.start()
    for i, copy in enumerate(copies):
        copy.wait()
        rows = pl.ds(i * block, block)
        o_ref[rows, :] = jnp.dot(xb[rows, :], w_ref[...], preferred_element_type=F32)


def base_rows(x, w, at, rows, block=128):
    k, n = w.shape
    return pl.pallas_call(
        functools.partial(base_kernel, at),
        in_specs=[HBM, VMEM],
        out_specs=VMEM,
        out_shape=jax.ShapeDtypeStruct((rows, n), F32),
        scratch_shapes=[pltpu.VMEM((rows, k), BF), pltpu.SemaphoreType.DMA((rows // block,))],
        compiler_params=params(36),
        cost_estimate=cost(1 << 20, 1 << 20),
        name="base",
    )(x, w)


def shrink_kernel(groups, has_sum, last, code_ref, x_ref, *refs):
    code = code_ref[...]
    refs = list(refs)
    total = None
    for count, places in groups:
        parts = [refs.pop(0)[...] for _ in range(count)]
        a = parts[0] if count == 1 else jnp.concatenate(parts, axis=0)
        p = lax.dot_general(x_ref[...], a, (((1,), (1,)), ((), ())), preferred_element_type=F32)
        for k, (j, i) in enumerate(places):
            term = jnp.where(code == owner(j, i), p[:, 128 * k : 128 * k + 128], 0.0)
            total = term if total is None else total + term
    if has_sum:
        total = total + refs.pop(0)[...]
    if not last:
        refs[0][...] = total
        return
    keep_ref, give_ref = refs
    half = total.shape[0] // 2
    folded = total + pltpu.roll(total, 64, 1)
    lane = lax.broadcasted_iota(jnp.int32, (half, 128), 1)
    packed = jnp.where(lane < 64, folded[:half], folded[half:])
    low, high = packed[: half // 2], packed[half // 2 :]
    core = lax.axis_index("tp") % 2
    keep_ref[...] = jnp.where(core == 0, low, high)
    give_ref[...] = jnp.where(core == 0, high, low)


def shrink(code, x, groups, total, last, name):
    m = x.shape[0]
    args = [code, x] + [a for parts, _ in groups for a in parts] + ([] if total is None else [total])
    rows = m // 4 if last else m
    shape = jax.ShapeDtypeStruct((rows, 128), F32)
    return pl.pallas_call(
        functools.partial(
            shrink_kernel, [(len(parts), places) for parts, places in groups], total is not None, last
        ),
        in_specs=[VMEM] * len(args),
        out_specs=[VMEM] * 2 if last else VMEM,
        out_shape=[shape] * 2 if last else shape,
        compiler_params=params(16),
        cost_estimate=cost(1 << 20, 1 << 20),
        name=name,
    )(*args)


def expand_kernel(pieces, code_ref, mine_ref, other_ref, *refs):
    base_refs, b_refs, o_ref = refs[: len(pieces)], refs[len(pieces) : -1], refs[-1]
    block = o_ref.shape[0]
    step = pl.program_id(0)
    code = code_ref[pl.ds(pl.multiple_of(step * block, block), block), :]
    mine = step % 2 == lax.axis_index("tp") % 2
    packed = jnp.where(mine, mine_ref[...].astype(F32), other_ref[...].astype(F32))
    lane = lax.broadcasted_iota(jnp.int32, packed.shape, 1)
    left = (lane < 64) == (step < 2)
    rows = jnp.where(left, packed, pltpu.roll(packed, 64, 1))
    delta = None
    for j, b_ref in zip(HOPS, b_refs):
        spread = jnp.concatenate(
            [jnp.where(code == owner(j, i), rows, 0.0).astype(BF) for i in HOPS], axis=1
        )
        d = jnp.dot(spread, b_ref[...], preferred_element_type=F32)
        delta = d if delta is None else delta + d
    delta = delta.astype(BF).astype(F32)
    at = 0
    for size, base_ref in zip(pieces, base_refs):

        @pl.when((step * block >= at) & (step * block < at + size))
        def _(at=at, base_ref=base_ref):
            row = pl.ds(pl.multiple_of(step * block - at, block), block)
            o_ref[...] = (base_ref[row, :] + adapter_scale * delta).astype(BF)

        at += size


def expand(code, mine, other, bases, parts):
    n = bases[0].shape[1]
    pieces = [a.shape[0] for a in bases]
    m = sum(pieces)
    block = m // 4
    args = [code, mine, other, *bases, *parts]
    return pl.pallas_call(
        functools.partial(expand_kernel, pieces),
        grid=(4,),
        in_specs=[VMEM] * len(args),
        out_specs=pl.BlockSpec((block, n), lambda i: (i, 0)),
        out_shape=jax.ShapeDtypeStruct((m, n), BF),
        compiler_params=params(12),
        cost_estimate=cost(2 * m * n * 2048, 6 * m * n),
        name="expand",
    )(*args)


def tie(*arrays):
    return lax.optimization_barrier(arrays)


def per_device(activations, token_adapter_index, query_matrix, down, up):
    down = jnp.swapaxes(down, 1, 2).reshape(128, -1)
    up = up.reshape(128, -1)
    m, width = activations.shape[0], down.shape[1]

    both = jnp.concatenate([down, up], axis=1)
    before, after, far = [first(both, d) for d in (1, -1, 2)]
    here, code = prepare(token_adapter_index, activations, width)
    before, after, here, code = tie(before, after, here, code)
    close = jnp.concatenate([down, before[:, :width], after[:, :width]], axis=0)
    a_before, a_after = second(close, 1), second(close, -1)
    d_far = far[:, :width]
    b_before, b_after = second(d_far, 1), second(d_far, -1)
    d_own = jnp.concatenate([close, d_far], axis=0)
    d_opposite = second(d_own, 2)
    u_own = jnp.concatenate([up, before[:, width:], after[:, width:], far[:, width:]], axis=0)

    base = [base_rows(activations, query_matrix, 0, m // 2)]
    total = shrink(code, here, [([d_own], [(0, i) for i in HOPS])], None, False, "shrink_own")
    a_before, a_after, total, base[0] = tie(a_before, a_after, total, base[0])
    groups = [([a], [(j, 0), (j, -1), (j, 1)]) for a, j in ((a_before, -1), (a_after, 1))]
    total = shrink(code, here, groups, total, False, "shrink_near")
    u_own = tie(u_own, base[0])[0]
    ups = [u_own] + [second(u_own, d) for d in (1, -1, 2)]
    b_before, b_after, d_opposite, total = tie(b_before, b_after, d_opposite, total)
    groups = [([b_before, b_after], [(-1, 2), (1, 2)]), ([d_opposite], [(2, i) for i in HOPS])]
    keep, give = shrink(code, here, groups, total, True, "shrink_far")
    keep = keep + other_core(give)
    for step in range(2):
        at = m // 2 + step * (m // 4)
        there, piece = tie(pair(keep, step), base_rows(activations, query_matrix, at, m // 4))
        keep = keep + there
        base.append(piece)
    mine, *ups = tie(keep.astype(BF), *ups)
    return expand(code, mine, other_core(mine), base, ups)


def solution(mesh):
    in_specs = (
        P("rep", None),
        P("rep", None),
        P(None, "tp"),
        P("rep", "tp", None),
        P("rep", None, "tp"),
    )
    return jax.shard_map(
        per_device, mesh=mesh, in_specs=in_specs, out_specs=P("rep", "tp"), check_vma=False
    )
```

```python
import functools

import jax
import jax.numpy as jnp
from jax import lax
from jax.experimental import pallas as pl
from jax.experimental.pallas import tpu as pltpu
from jax.sharding import PartitionSpec as P

BF, F32 = jnp.bfloat16, jnp.float32
AXES = ("rep", "tp")
RING = 4
HOPS = (0, -1, 1, 2)
adapter_scale = 0.5


def device_of(x, y, z, c):
    return (z % RING * RING + x % RING) * 2 * RING + y % RING * 2 + c


def every(f):
    return [
        (device_of(x, y, z, c), device_of(*f(x, y, z, c)))
        for z in range(RING)
        for x in range(RING)
        for y in range(RING)
        for c in range(2)
    ]


def first(a, d):
    return lax.ppermute(
        a, AXES, every(lambda x, y, z, c: (x, y, z + d, c) if c else (x + d, y, z, c))
    )


def second(a, d):
    return lax.ppermute(
        a, AXES, every(lambda x, y, z, c: (x + d, y, z, c) if c else (x, y, z + d, c))
    )


def other_core(a):
    return lax.ppermute(a, AXES, every(lambda x, y, z, c: (x, y, z, 1 - c)))


def pair(a, step):
    def to(x, y, z, c):
        return (x, (y ^ 1) if (c + step) % 2 == 0 else (3 - y), z, c)

    return lax.ppermute(a, AXES, every(to))


def params(mib):
    return pltpu.CompilerParams(vmem_limit_bytes=mib << 20)


def cost(flops, moved):
    return pl.CostEstimate(flops=flops, bytes_accessed=moved, transcendentals=0)


VMEM = pl.BlockSpec(memory_space=pltpu.VMEM)
HBM = pl.BlockSpec(memory_space=pltpu.HBM)


def owner(j, i):
    rep, core = lax.axis_index("rep"), lax.axis_index("tp") % 2
    dz, dx = jnp.where(core == 0, j, i), jnp.where(core == 0, i, j)
    return (rep // RING + dz + RING) % RING * RING + (rep % RING + dx + RING) % RING


def prep_kernel(ident_ref, x_ref, here_ref, code_ref, sem):
    width = here_ref.shape[1]
    at = pl.multiple_of(lax.axis_index("tp") * width, width)
    copy = pltpu.make_async_copy(x_ref.at[:, pl.ds(at, width)], here_ref, sem)
    copy.start()
    side = lax.broadcasted_iota(jnp.int32, (128, 128), 1) // 64
    for r in range(ident_ref.shape[0]):
        ident = jnp.broadcast_to(ident_ref[r : r + 1, :], (128, 128)).T
        code_ref[128 * r : 128 * r + 128, :] = jnp.where((ident & 1) == side, ident >> 1, -1)
    copy.wait()


def prepare(ident, x, width):
    m = x.shape[0]
    return pl.pallas_call(
        prep_kernel,
        in_specs=[VMEM, HBM],
        out_specs=[VMEM, VMEM],
        out_shape=[
            jax.ShapeDtypeStruct((m, width), BF),
            jax.ShapeDtypeStruct((m, 128), jnp.int32),
        ],
        scratch_shapes=[pltpu.SemaphoreType.DMA],
        compiler_params=params(50),
        cost_estimate=cost(0, 1 << 20),
        name="prepare",
    )(ident.reshape(m // 128, 128), x)


def base_kernel(at, x_ref, w_ref, o_ref, xb, sems):
    count = sems.shape[0]
    block = xb.shape[0] // count
    copies = []
    for i in range(count):
        rows = pl.ds(i * block, block)
        copies.append(
            pltpu.make_async_copy(x_ref.at[pl.ds(at + i * block, block)], xb.at[rows], sems.at[i])
        )
    for copy in copies:
        copy.start()
    for i, copy in enumerate(copies):
        copy.wait()
        rows = pl.ds(i * block, block)
        o_ref[rows, :] = jnp.dot(xb[rows, :], w_ref[...], preferred_element_type=F32)


def base_rows(x, w, at, rows, block=256):
    k, n = w.shape
    return pl.pallas_call(
        functools.partial(base_kernel, at),
        in_specs=[HBM, VMEM],
        out_specs=VMEM,
        out_shape=jax.ShapeDtypeStruct((rows, n), F32),
        scratch_shapes=[pltpu.VMEM((rows, k), BF), pltpu.SemaphoreType.DMA((rows // block,))],
        compiler_params=params(36),
        cost_estimate=cost(1 << 20, 1 << 20),
        name="base",
    )(x, w)


def shrink_kernel(groups, has_sum, last, code_ref, x_ref, *refs):
    code = code_ref[...]
    refs = list(refs)
    total = None
    for count, places in groups:
        parts = [refs.pop(0)[...] for _ in range(count)]
        a = parts[0] if count == 1 else jnp.concatenate(parts, axis=0)
        p = lax.dot_general(x_ref[...], a, (((1,), (1,)), ((), ())), preferred_element_type=F32)
        for k, (j, i) in enumerate(places):
            term = jnp.where(code == owner(j, i), p[:, 128 * k : 128 * k + 128], 0.0)
            total = term if total is None else total + term
    if has_sum:
        total = total + refs.pop(0)[...]
    if not last:
        refs[0][...] = total
        return
    keep_ref, give_ref = refs
    half = total.shape[0] // 2
    folded = total + pltpu.roll(total, 64, 1)
    lane = lax.broadcasted_iota(jnp.int32, (half, 128), 1)
    packed = jnp.where(lane < 64, folded[:half], folded[half:])
    low, high = packed[: half // 2], packed[half // 2 :]
    core = lax.axis_index("tp") % 2
    keep_ref[...] = jnp.where(core == 0, low, high)
    give_ref[...] = jnp.where(core == 0, high, low)


def shrink(code, x, groups, total, last, name, weight=1 << 20):
    m = x.shape[0]
    args = [code, x] + [a for parts, _ in groups for a in parts] + ([] if total is None else [total])
    rows = m // 4 if last else m
    shape = jax.ShapeDtypeStruct((rows, 128), F32)
    return pl.pallas_call(
        functools.partial(
            shrink_kernel, [(len(parts), places) for parts, places in groups], total is not None, last
        ),
        in_specs=[VMEM] * len(args),
        out_specs=[VMEM] * 2 if last else VMEM,
        out_shape=[shape] * 2 if last else shape,
        compiler_params=params(16),
        cost_estimate=cost(weight, 1 << 20),
        name=name,
    )(*args)


def expand_kernel(pieces, code_ref, mine_ref, other_ref, *refs):
    base_refs, b_refs, o_ref = refs[: len(pieces)], refs[len(pieces) : -1], refs[-1]
    block = o_ref.shape[0]
    step = pl.program_id(0)
    code = code_ref[pl.ds(pl.multiple_of(step * block, block), block), :]
    core = lax.axis_index("tp") % 2
    mine, other = mine_ref[...].astype(F32), other_ref[...].astype(F32)
    packed = jnp.concatenate(
        [jnp.where(core == 0, mine, other), jnp.where(core == 0, other, mine)], axis=0
    )
    lane = lax.broadcasted_iota(jnp.int32, packed.shape, 1)
    left = (lane < 64) == (step == 0)
    rows = jnp.where(left, packed, pltpu.roll(packed, 64, 1))
    delta = None
    for j, b_ref in zip(HOPS, b_refs):
        spread = jnp.concatenate(
            [jnp.where(code == owner(j, i), rows, 0.0).astype(BF) for i in HOPS], axis=1
        )
        d = jnp.dot(spread, b_ref[...], preferred_element_type=F32)
        delta = d if delta is None else delta + d
    delta = delta.astype(BF).astype(F32)
    at = 0
    for size, base_ref in zip(pieces, base_refs):

        @pl.when(step == at // block)
        def _(row=pl.ds(at % block, size), base_ref=base_ref):
            o_ref[row, :] = (base_ref[...] + adapter_scale * delta[row.start : row.start + size]).astype(BF)

        at += size


def expand(code, mine, other, bases, parts):
    n = bases[0].shape[1]
    pieces = [a.shape[0] for a in bases]
    m = sum(pieces)
    block = m // 2
    args = [code, mine, other, *bases, *parts]
    return pl.pallas_call(
        functools.partial(expand_kernel, pieces),
        grid=(2,),
        in_specs=[VMEM] * len(args),
        out_specs=pl.BlockSpec((block, n), lambda i: (i, 0)),
        out_shape=jax.ShapeDtypeStruct((m, n), BF),
        compiler_params=params(12),
        cost_estimate=cost(2 * m * n * 2048, 6 * m * n),
        name="expand",
    )(*args)


def tie(*arrays):
    return lax.optimization_barrier(arrays)


def per_device(activations, token_adapter_index, query_matrix, down, up):
    down = jnp.swapaxes(down, 1, 2).reshape(128, -1)
    up = up.reshape(128, -1)
    m, width = activations.shape[0], down.shape[1]

    both = jnp.concatenate([down, up], axis=1)
    before, after, far = [first(both, d) for d in (1, -1, 2)]
    here, code = prepare(token_adapter_index, activations, width)
    before, after, here, code = tie(before, after, here, code)
    close = jnp.concatenate([down, before[:, :width], after[:, :width]], axis=0)
    a_before, a_after = second(close, 1), second(close, -1)
    d_far = far[:, :width]
    b_before, b_after = second(d_far, 1), second(d_far, -1)
    d_own = jnp.concatenate([close, d_far], axis=0)
    d_opposite = second(d_own, 2)
    u_own = jnp.concatenate([up, before[:, width:], after[:, width:], far[:, width:]], axis=0)

    base = [base_rows(activations, query_matrix, 0, m // 2)]
    total = shrink(code, here, [([d_own], [(0, i) for i in HOPS])], None, False, "shrink_own")
    a_before, a_after, total, base[0] = tie(a_before, a_after, total, base[0])
    groups = [([a], [(j, 0), (j, -1), (j, 1)]) for a, j in ((a_before, -1), (a_after, 1))]
    total = shrink(code, here, groups, total, False, "shrink_near", 5000000000)
    u_own = tie(u_own, base[0])[0]
    ups = [u_own] + [second(u_own, d) for d in (1, -1, 2)]
    b_before, b_after, d_opposite, total = tie(b_before, b_after, d_opposite, total)
    groups = [([b_before, b_after], [(-1, 2), (1, 2)]), ([d_opposite], [(2, i) for i in HOPS])]
    keep, give = shrink(code, here, groups, total, True, "shrink_far")
    keep = keep + other_core(give)
    for step in range(2):
        at = m // 2 + step * (m // 4)
        there, piece = tie(pair(keep, step), base_rows(activations, query_matrix, at, m // 4))
        keep = keep + there
        base.append(piece)
        if step == 0:
            keep, *ups = tie(keep, *ups)
    mine = keep.astype(BF)
    return expand(code, mine, other_core(mine), base, ups)


def solution(mesh):
    in_specs = (
        P("rep", None),
        P("rep", None),
        P(None, "tp"),
        P("rep", "tp", None),
        P("rep", None, "tp"),
    )
    return jax.shard_map(
        per_device, mesh=mesh, in_specs=in_specs, out_specs=P("rep", "tp"), check_vma=False
    )
```

```python
import functools

import jax
import jax.numpy as jnp
from jax import lax
from jax.experimental import pallas as pl
from jax.experimental.pallas import tpu as pltpu
from jax.sharding import PartitionSpec as P

BF, F32 = jnp.bfloat16, jnp.float32
AXES = ("rep", "tp")
RING = 4
HOPS = (0, -1, 1, 2)
adapter_scale = 0.5


def device_of(x, y, z, c):
    return (z % RING * RING + x % RING) * 2 * RING + y % RING * 2 + c


def every(f):
    return [
        (device_of(x, y, z, c), device_of(*f(x, y, z, c)))
        for z in range(RING)
        for x in range(RING)
        for y in range(RING)
        for c in range(2)
    ]


def first(a, d):
    return lax.ppermute(
        a, AXES, every(lambda x, y, z, c: (x, y, z + d, c) if c else (x + d, y, z, c))
    )


def second(a, d):
    return lax.ppermute(
        a, AXES, every(lambda x, y, z, c: (x + d, y, z, c) if c else (x, y, z + d, c))
    )


def other_core(a):
    return lax.ppermute(a, AXES, every(lambda x, y, z, c: (x, y, z, 1 - c)))


def pair(a, step):
    def to(x, y, z, c):
        return (x, (y ^ 1) if (c + step) % 2 == 0 else (3 - y), z, c)

    return lax.ppermute(a, AXES, every(to))


def params(mib):
    return pltpu.CompilerParams(vmem_limit_bytes=mib << 20)


def cost(flops, moved):
    return pl.CostEstimate(flops=flops, bytes_accessed=moved, transcendentals=0)


VMEM = pl.BlockSpec(memory_space=pltpu.VMEM)
HBM = pl.BlockSpec(memory_space=pltpu.HBM)


def owner(j, i):
    rep, core = lax.axis_index("rep"), lax.axis_index("tp") % 2
    dz, dx = jnp.where(core == 0, j, i), jnp.where(core == 0, i, j)
    return (rep // RING + dz + RING) % RING * RING + (rep % RING + dx + RING) % RING


def prep_kernel(ident_ref, x_ref, here_ref, half_ref, code_ref, sems):
    width, rows = here_ref.shape[1], half_ref.shape[0]
    at = pl.multiple_of(lax.axis_index("tp") * width, width)
    here = pltpu.make_async_copy(x_ref.at[:, pl.ds(at, width)], here_ref, sems.at[0])
    half = pltpu.make_async_copy(x_ref.at[pl.ds(0, rows)], half_ref, sems.at[1])
    here.start()
    half.start()
    side = lax.broadcasted_iota(jnp.int32, (128, 128), 1) // 64
    for r in range(ident_ref.shape[0]):
        ident = jnp.broadcast_to(ident_ref[r : r + 1, :], (128, 128)).T
        code_ref[128 * r : 128 * r + 128, :] = jnp.where((ident & 1) == side, ident >> 1, -1)
    here.wait()
    half.wait()


def prepare(ident, x, width):
    m, k = x.shape
    return pl.pallas_call(
        prep_kernel,
        in_specs=[VMEM, HBM],
        out_specs=[VMEM] * 3,
        out_shape=[
            jax.ShapeDtypeStruct((m, width), BF),
            jax.ShapeDtypeStruct((m // 2, k), BF),
            jax.ShapeDtypeStruct((m, 128), jnp.int32),
        ],
        scratch_shapes=[pltpu.SemaphoreType.DMA((2,))],
        compiler_params=params(28),
        cost_estimate=cost(0, 1 << 20),
        name="prepare",
    )(ident.reshape(m // 128, 128), x)


def base_kernel(half_ref, x_ref, w_ref, o_ref, xb, sems):
    half, block = xb.shape[0], 256
    count = half // block
    copies = [
        pltpu.make_async_copy(
            x_ref.at[pl.ds(half + i * block, block)], xb.at[pl.ds(i * block, block)], sems.at[i]
        )
        for i in range(count)
    ]
    for copy in copies:
        copy.start()

    def multiply(rows, at):
        o_ref[pl.ds(at, block), :] = jnp.dot(rows, w_ref[...], preferred_element_type=F32)

    def first_rows(i, _):
        at = pl.multiple_of(i * block, block)
        multiply(half_ref[pl.ds(at, block), :], at)
        return 0

    def other_rows(i, _):
        at = pl.multiple_of(i * block, block)
        multiply(xb[pl.ds(at, block), :], half + at)
        return 0

    lax.fori_loop(0, count, first_rows, 0)
    for copy in copies:
        copy.wait()
    lax.fori_loop(0, count, other_rows, 0)


def base_product(half, x, w):
    (m, k), n = x.shape, w.shape[1]
    return pl.pallas_call(
        base_kernel,
        in_specs=[VMEM, HBM, VMEM],
        out_specs=VMEM,
        out_shape=jax.ShapeDtypeStruct((m, n), F32),
        scratch_shapes=[pltpu.VMEM((m // 2, k), BF), pltpu.SemaphoreType.DMA((m // 512,))],
        compiler_params=params(22),
        cost_estimate=cost(1 << 20, 1 << 20),
        name="base",
    )(half, x, w)


def shrink_kernel(groups, has_sum, last, code_ref, x_ref, *refs):
    code = code_ref[...]
    refs = list(refs)
    total = None
    for count, places in groups:
        parts = [refs.pop(0)[...] for _ in range(count)]
        a = parts[0] if count == 1 else jnp.concatenate(parts, axis=0)
        p = lax.dot_general(x_ref[...], a, (((1,), (1,)), ((), ())), preferred_element_type=F32)
        for k, (j, i) in enumerate(places):
            term = jnp.where(code == owner(j, i), p[:, 128 * k : 128 * k + 128], 0.0)
            total = term if total is None else total + term
    if has_sum:
        total = total + refs.pop(0)[...]
    if not last:
        refs[0][...] = total
        return
    keep_ref, give_ref = refs
    half = total.shape[0] // 2
    folded = total + pltpu.roll(total, 64, 1)
    lane = lax.broadcasted_iota(jnp.int32, (half, 128), 1)
    packed = jnp.where(lane < 64, folded[:half], folded[half:])
    low, high = packed[: half // 2], packed[half // 2 :]
    core = lax.axis_index("tp") % 2
    keep_ref[...] = jnp.where(core == 0, low, high)
    give_ref[...] = jnp.where(core == 0, high, low)


def shrink(code, x, groups, total, last, name, weight=1 << 20):
    m = x.shape[0]
    args = [code, x] + [a for parts, _ in groups for a in parts] + ([] if total is None else [total])
    rows = m // 4 if last else m
    shape = jax.ShapeDtypeStruct((rows, 128), F32)
    return pl.pallas_call(
        functools.partial(
            shrink_kernel, [(len(parts), places) for parts, places in groups], total is not None, last
        ),
        in_specs=[VMEM] * len(args),
        out_specs=[VMEM] * 2 if last else VMEM,
        out_shape=[shape] * 2 if last else shape,
        compiler_params=params(16),
        cost_estimate=cost(weight, 1 << 20),
        name=name,
    )(*args)


def expand_kernel(groups, code_ref, mine_ref, other_ref, base_ref, *refs):
    b_refs, o_ref = refs[:-1], refs[-1]
    block = o_ref.shape[0]
    step = pl.program_id(0)
    here = pl.ds(pl.multiple_of(step * block, block), block)
    code = code_ref[here, :]
    core = lax.axis_index("tp") % 2
    mine, other = mine_ref[...].astype(F32), other_ref[...].astype(F32)
    packed = jnp.concatenate(
        [jnp.where(core == 0, mine, other), jnp.where(core == 0, other, mine)], axis=0
    )
    lane = lax.broadcasted_iota(jnp.int32, packed.shape, 1)
    left = (lane < 64) == (step == 0)
    rows = jnp.where(left, packed, pltpu.roll(packed, 64, 1))
    delta = None
    for places, b_ref in zip(groups, b_refs):
        spread = jnp.concatenate(
            [jnp.where(code == owner(j, i), rows, 0.0).astype(BF) for j, i in places], axis=1
        )
        d = jnp.dot(spread, b_ref[...], preferred_element_type=F32)
        delta = d if delta is None else delta + d
    delta = delta.astype(BF).astype(F32)
    o_ref[...] = (base_ref[here, :] + adapter_scale * delta).astype(BF)


def expand(code, mine, other, base, parts):
    m, n = base.shape
    block = m // 2
    args = [code, mine, other, base] + [a for a, _ in parts]
    return pl.pallas_call(
        functools.partial(expand_kernel, [places for _, places in parts]),
        grid=(2,),
        in_specs=[VMEM] * len(args),
        out_specs=pl.BlockSpec((block, n), lambda i: (i, 0)),
        out_shape=jax.ShapeDtypeStruct((m, n), BF),
        compiler_params=params(12),
        cost_estimate=cost(2 * m * n * 2048, 6 * m * n),
        name="expand",
    )(*args)


def tie(*arrays):
    return lax.optimization_barrier(arrays)


def forward(before, after):
    half = before.shape[0] // 2
    return second(before[:half], 1), second(after[half:], -1)


def per_device(activations, token_adapter_index, query_matrix, down, up):
    down = jnp.swapaxes(down, 1, 2).reshape(128, -1)
    up = up.reshape(128, -1)
    width = down.shape[1]
    row = lambda j, hops=HOPS: [(j, i) for i in hops]

    both = jnp.concatenate([down, up], axis=1)
    near = [first(both, d) for d in (1, -1, 2)]
    here, half, code = prepare(token_adapter_index, activations, width)
    near, here, half, code = tie(near, here, half, code)
    d_own = jnp.concatenate([down] + [a[:, :width] for a in near], axis=0)
    u_own = jnp.concatenate([up] + [a[:, width:] for a in near], axis=0)

    d_own, u_own = tie(d_own, u_own)
    d_before, d_after = second(d_own, 1), second(d_own, -1)
    base = base_product(half, activations, query_matrix)
    d_before, d_after, base = tie(d_before, d_after, base)
    d_far = forward(d_before, d_after)
    groups = [([d_own], row(0)), ([d_before], row(-1)), ([d_after], row(1))]
    total = shrink(code, here, groups, None, False, "shrink_near")
    u_before, u_after = second(u_own, 1), second(u_own, -1)
    *d_far, total = tie(*d_far, total)
    keep, give = shrink(code, here, [(d_far, row(2))], total, True, "shrink_far")
    keep = keep + other_core(give)
    keep, u_before, u_after = tie(keep, u_before, u_after)
    u_far = forward(u_before, u_after)
    keep = keep + pair(keep, 0)
    keep = keep + pair(keep, 1)
    mine = keep.astype(BF)
    parts = [(u_own, row(0)), (u_before, row(-1)), (u_after, row(1))]
    parts += [(a, row(2, hops)) for a, hops in zip(u_far, (HOPS[:2], HOPS[2:]))]
    return expand(code, mine, other_core(mine), base, parts)


def solution(mesh):
    in_specs = (
        P("rep", None),
        P("rep", None),
        P(None, "tp"),
        P("rep", "tp", None),
        P("rep", None, "tp"),
    )
    return jax.shard_map(
        per_device, mesh=mesh, in_specs=in_specs, out_specs=P("rep", "tp"), check_vma=False
    )
```

```python
import functools

import jax
import jax.numpy as jnp
from jax import lax
from jax.experimental import pallas as pl
from jax.experimental.pallas import tpu as pltpu
from jax.sharding import PartitionSpec as P

BF, F32 = jnp.bfloat16, jnp.float32
AXES = ("rep", "tp")
RING = 4
HOPS = (0, -1, 1, 2)
adapter_scale = 0.5


def device_of(x, y, z, c):
    return (z % RING * RING + x % RING) * 2 * RING + y % RING * 2 + c


def every(f):
    return [
        (device_of(x, y, z, c), device_of(*f(x, y, z, c)))
        for z in range(RING)
        for x in range(RING)
        for y in range(RING)
        for c in range(2)
    ]


def first(a, d):
    return lax.ppermute(
        a, AXES, every(lambda x, y, z, c: (x, y, z + d, c) if c else (x + d, y, z, c))
    )


def second(a, d):
    return lax.ppermute(
        a, AXES, every(lambda x, y, z, c: (x + d, y, z, c) if c else (x, y, z + d, c))
    )


def other_core(a):
    return lax.ppermute(a, AXES, every(lambda x, y, z, c: (x, y, z, 1 - c)))


def pair(a, step):
    def to(x, y, z, c):
        return (x, (y ^ 1) if (c + step) % 2 == 0 else (3 - y), z, c)

    return lax.ppermute(a, AXES, every(to))


def params(mib):
    return pltpu.CompilerParams(vmem_limit_bytes=mib << 20)


def cost(flops, moved):
    return pl.CostEstimate(flops=flops, bytes_accessed=moved, transcendentals=0)


VMEM = pl.BlockSpec(memory_space=pltpu.VMEM)
HBM = pl.BlockSpec(memory_space=pltpu.HBM)


def owner(j, i):
    rep, core = lax.axis_index("rep"), lax.axis_index("tp") % 2
    dz, dx = jnp.where(core == 0, j, i), jnp.where(core == 0, i, j)
    return (rep // RING + dz + RING) % RING * RING + (rep % RING + dx + RING) % RING


def prep_kernel(ident_ref, x_ref, here_ref, half_ref, code_ref, sems):
    width, rows = here_ref.shape[1], half_ref.shape[0]
    at = pl.multiple_of(lax.axis_index("tp") * width, width)
    here = pltpu.make_async_copy(x_ref.at[:, pl.ds(at, width)], here_ref, sems.at[0])
    half = pltpu.make_async_copy(x_ref.at[pl.ds(0, rows)], half_ref, sems.at[1])
    here.start()
    half.start()
    side = lax.broadcasted_iota(jnp.int32, (128, 128), 1) // 64
    for r in range(ident_ref.shape[0]):
        ident = jnp.broadcast_to(ident_ref[r : r + 1, :], (128, 128)).T
        code_ref[128 * r : 128 * r + 128, :] = jnp.where((ident & 1) == side, ident >> 1, -1)
    here.wait()
    half.wait()


def prepare(ident, x, width):
    m, k = x.shape
    return pl.pallas_call(
        prep_kernel,
        in_specs=[VMEM, HBM],
        out_specs=[VMEM] * 3,
        out_shape=[
            jax.ShapeDtypeStruct((m, width), BF),
            jax.ShapeDtypeStruct((m // 2, k), BF),
            jax.ShapeDtypeStruct((m, 128), jnp.int32),
        ],
        scratch_shapes=[pltpu.SemaphoreType.DMA((2,))],
        compiler_params=params(28),
        cost_estimate=cost(0, 1 << 20),
        name="prepare",
    )(ident.reshape(m // 128, 128), x)


def multiply(x_ref, w_ref, o_ref, block=256):
    def rows(i, _):
        at = pl.ds(pl.multiple_of(i * block, block), block)
        o_ref[at, :] = jnp.dot(x_ref[at, :], w_ref[...], preferred_element_type=F32)
        return 0

    lax.fori_loop(0, x_ref.shape[0] // block, rows, 0)


def base_kernel(half_ref, w_ref, x_ref, o_ref, rest_ref, sem):
    rows = rest_ref.shape[0]
    copy = pltpu.make_async_copy(x_ref.at[pl.ds(rows, rows)], rest_ref, sem)
    copy.start()
    multiply(half_ref, w_ref, o_ref)
    copy.wait()


def base_first(half, w, x):
    rows, n = half.shape[0], w.shape[1]
    return pl.pallas_call(
        base_kernel,
        in_specs=[VMEM, VMEM, HBM],
        out_specs=[VMEM, VMEM],
        out_shape=[jax.ShapeDtypeStruct((rows, n), F32), jax.ShapeDtypeStruct(half.shape, BF)],
        scratch_shapes=[pltpu.SemaphoreType.DMA],
        compiler_params=params(28),
        cost_estimate=cost(5000000000, 1 << 20),
        name="base_first",
    )(half, w, x)


def base_second(rest, w):
    return pl.pallas_call(
        multiply,
        in_specs=[VMEM, VMEM],
        out_specs=VMEM,
        out_shape=jax.ShapeDtypeStruct((rest.shape[0], w.shape[1]), F32),
        compiler_params=params(12),
        cost_estimate=cost(5000000000, 1 << 20),
        name="base_second",
    )(rest, w)


def shrink_kernel(groups, has_sum, last, code_ref, x_ref, *refs):
    code = code_ref[...]
    refs = list(refs)
    total = None
    for count, places in groups:
        parts = [refs.pop(0)[...] for _ in range(count)]
        a = parts[0] if count == 1 else jnp.concatenate(parts, axis=0)
        p = lax.dot_general(x_ref[...], a, (((1,), (1,)), ((), ())), preferred_element_type=F32)
        for k, (j, i) in enumerate(places):
            term = jnp.where(code == owner(j, i), p[:, 128 * k : 128 * k + 128], 0.0)
            total = term if total is None else total + term
    if has_sum:
        total = total + refs.pop(0)[...]
    if not last:
        refs[0][...] = total
        return
    keep_ref, give_ref = refs
    half = total.shape[0] // 2
    folded = total + pltpu.roll(total, 64, 1)
    lane = lax.broadcasted_iota(jnp.int32, (half, 128), 1)
    packed = jnp.where(lane < 64, folded[:half], folded[half:])
    low, high = packed[: half // 2], packed[half // 2 :]
    core = lax.axis_index("tp") % 2
    keep_ref[...] = jnp.where(core == 0, low, high)
    give_ref[...] = jnp.where(core == 0, high, low)


def shrink(code, x, groups, total, last, name, weight=1 << 20):
    m = x.shape[0]
    args = [code, x] + [a for parts, _ in groups for a in parts] + ([] if total is None else [total])
    rows = m // 4 if last else m
    shape = jax.ShapeDtypeStruct((rows, 128), F32)
    return pl.pallas_call(
        functools.partial(
            shrink_kernel, [(len(parts), places) for parts, places in groups], total is not None, last
        ),
        in_specs=[VMEM] * len(args),
        out_specs=[VMEM] * 2 if last else VMEM,
        out_shape=[shape] * 2 if last else shape,
        compiler_params=params(16),
        cost_estimate=cost(weight, 1 << 20),
        name=name,
    )(*args)


def expand_kernel(groups, code_ref, mine_ref, other_ref, top_ref, bottom_ref, *refs):
    b_refs, o_ref = refs[:-1], refs[-1]
    block = o_ref.shape[0]
    step = pl.program_id(0)
    here = pl.ds(pl.multiple_of(step * block, block), block)
    code = code_ref[here, :]
    core = lax.axis_index("tp") % 2
    mine, other = mine_ref[...].astype(F32), other_ref[...].astype(F32)
    packed = jnp.concatenate(
        [jnp.where(core == 0, mine, other), jnp.where(core == 0, other, mine)], axis=0
    )
    lane = lax.broadcasted_iota(jnp.int32, packed.shape, 1)
    left = (lane < 64) == (step == 0)
    rows = jnp.where(left, packed, pltpu.roll(packed, 64, 1))
    delta = None
    for places, b_ref in zip(groups, b_refs):
        spread = jnp.concatenate(
            [jnp.where(code == owner(j, i), rows, 0.0).astype(BF) for j, i in places], axis=1
        )
        d = jnp.dot(spread, b_ref[...], preferred_element_type=F32)
        delta = d if delta is None else delta + d
    delta = delta.astype(BF).astype(F32)
    for i, base_ref in enumerate((top_ref, bottom_ref)):

        @pl.when(step == i)
        def _(base_ref=base_ref):
            o_ref[...] = (base_ref[...] + adapter_scale * delta).astype(BF)


def expand(code, mine, other, base, parts):
    block, n = base[0].shape
    m = 2 * block
    args = [code, mine, other, *base] + [a for a, _ in parts]
    return pl.pallas_call(
        functools.partial(expand_kernel, [places for _, places in parts]),
        grid=(2,),
        in_specs=[VMEM] * len(args),
        out_specs=pl.BlockSpec((block, n), lambda i: (i, 0)),
        out_shape=jax.ShapeDtypeStruct((m, n), BF),
        compiler_params=params(12),
        cost_estimate=cost(2 * m * n * 2048, 6 * m * n),
        name="expand",
    )(*args)


def tie(*arrays):
    return lax.optimization_barrier(arrays)


def per_device(activations, token_adapter_index, query_matrix, down, up):
    down = jnp.swapaxes(down, 1, 2).reshape(128, -1)
    up = up.reshape(128, -1)
    width = down.shape[1]
    row = lambda j, hops=HOPS: [(j, i) for i in hops]

    both = jnp.concatenate([down, up], axis=1)
    before, after = first(both, 1), first(both, -1)
    here, half, code = prepare(token_adapter_index, activations, width)
    both, here, half, code = tie(both, here, half, code)
    far = first(both, 2)
    close = jnp.concatenate([down, before[:, :width], after[:, :width]], axis=0)
    a_before, a_after = second(close, 1), second(close, -1)
    base, rest = base_first(half, query_matrix, activations)
    far, base, rest = tie(far, base, rest)
    d_far = far[:, :width]
    u_own = jnp.concatenate([up] + [a[:, width:] for a in (before, after, far)], axis=0)
    b_before, b_after = second(d_far, 1), second(d_far, -1)
    d_own = jnp.concatenate([close, d_far], axis=0)
    base = [base, base_second(rest, query_matrix)]
    a_before, a_after, b_before, b_after, base[1] = tie(a_before, a_after, b_before, b_after, base[1])

    d_two = [second(a_before[:256], 1), second(jnp.concatenate([a_after[256:], b_after]), -1)]
    groups = [([d_own], row(0)), ([a_before, b_before], row(-1)), ([a_after, b_after], row(1))]
    total = shrink(code, here, groups, None, False, "shrink_near")
    total, u_own = tie(total, u_own)
    u_before, u_after = second(u_own, 1), second(u_own, -1)
    *d_two, total = tie(*d_two, total)
    keep, give = shrink(code, here, [(d_two, row(2))], total, True, "shrink_far")
    keep = keep + other_core(give)
    keep, u_before, u_after = tie(keep, u_before, u_after)
    u_two = [second(u_before[:256], 1), second(u_after[256:], -1)]
    keep = keep + pair(keep, 0)
    keep = keep + pair(keep, 1)
    mine, *u_two = tie(keep.astype(BF), *u_two)
    parts = [(u_own, row(0)), (u_before, row(-1)), (u_after, row(1))]
    parts += [(a, row(2, hops)) for a, hops in zip(u_two, (HOPS[:2], HOPS[2:]))]
    return expand(code, mine, other_core(mine), base, parts)


def solution(mesh):
    in_specs = (
        P("rep", None),
        P("rep", None),
        P(None, "tp"),
        P("rep", "tp", None),
        P("rep", None, "tp"),
    )
    return jax.shard_map(
        per_device, mesh=mesh, in_specs=in_specs, out_specs=P("rep", "tp"), check_vma=False
    )
```

```python
import functools

import jax
import jax.numpy as jnp
from jax import lax
from jax.experimental import pallas as pl
from jax.experimental.pallas import tpu as pltpu
from jax.sharding import PartitionSpec as P

BF, F32 = jnp.bfloat16, jnp.float32
AXES = ("rep", "tp")
RING = 4
HOPS = (0, -1, 1, 2)
adapter_scale = 0.5


def device_of(x, y, z, c):
    return (z % RING * RING + x % RING) * 2 * RING + y % RING * 2 + c


def every(f):
    return [
        (device_of(x, y, z, c), device_of(*f(x, y, z, c)))
        for z in range(RING)
        for x in range(RING)
        for y in range(RING)
        for c in range(2)
    ]


def first(a, d):
    return lax.ppermute(
        a, AXES, every(lambda x, y, z, c: (x, y, z + d, c) if c else (x + d, y, z, c))
    )


def second(a, d):
    return lax.ppermute(
        a, AXES, every(lambda x, y, z, c: (x + d, y, z, c) if c else (x, y, z + d, c))
    )


def other_core(a):
    return lax.ppermute(a, AXES, every(lambda x, y, z, c: (x, y, z, 1 - c)))


def pair(a, step):
    def to(x, y, z, c):
        return (x, (y ^ 1) if (c + step) % 2 == 0 else (3 - y), z, c)

    return lax.ppermute(a, AXES, every(to))


def params(mib):
    return pltpu.CompilerParams(vmem_limit_bytes=mib << 20)


def cost(flops, moved):
    return pl.CostEstimate(flops=flops, bytes_accessed=moved, transcendentals=0)


VMEM = pl.BlockSpec(memory_space=pltpu.VMEM)
HBM = pl.BlockSpec(memory_space=pltpu.HBM)


def owner(j, i):
    rep, core = lax.axis_index("rep"), lax.axis_index("tp") % 2
    dz, dx = jnp.where(core == 0, j, i), jnp.where(core == 0, i, j)
    return (rep // RING + dz + RING) % RING * RING + (rep % RING + dx + RING) % RING


def code_kernel(ident_ref, code_ref):
    side = lax.broadcasted_iota(jnp.int32, (128, 128), 1) // 64
    for r in range(ident_ref.shape[0]):
        ident = jnp.broadcast_to(ident_ref[r : r + 1, :], (128, 128)).T
        code_ref[128 * r : 128 * r + 128, :] = jnp.where((ident & 1) == side, ident >> 1, -1)


def mask_code(ident):
    m = ident.shape[0]
    return pl.pallas_call(
        code_kernel,
        in_specs=[VMEM],
        out_specs=VMEM,
        out_shape=jax.ShapeDtypeStruct((m, 128), jnp.int32),
        compiler_params=params(2),
        cost_estimate=cost(1 << 20, 1 << 20),
        name="mask_code",
    )(ident.reshape(m // 128, 128))


def fetch_kernel(x_ref, here_ref, half_ref, sems):
    width, rows = here_ref.shape[1], half_ref.shape[0]
    at = pl.multiple_of(lax.axis_index("tp") * width, width)
    here = pltpu.make_async_copy(x_ref.at[:, pl.ds(at, width)], here_ref, sems.at[0])
    half = pltpu.make_async_copy(x_ref.at[pl.ds(0, rows)], half_ref, sems.at[1])
    here.start()
    half.start()
    here.wait()
    half.wait()


def fetch(x, width):
    m, k = x.shape
    return pl.pallas_call(
        fetch_kernel,
        in_specs=[HBM],
        out_specs=[VMEM] * 2,
        out_shape=[jax.ShapeDtypeStruct((m, width), BF), jax.ShapeDtypeStruct((m // 2, k), BF)],
        scratch_shapes=[pltpu.SemaphoreType.DMA((2,))],
        compiler_params=params(28),
        cost_estimate=cost(1000000, 1 << 20),
        name="fetch",
    )(x)


def multiply(x_ref, w_ref, o_ref, block=256):
    def rows(i, _):
        at = pl.ds(pl.multiple_of(i * block, block), block)
        o_ref[at, :] = jnp.dot(x_ref[at, :], w_ref[...], preferred_element_type=F32)
        return 0

    lax.fori_loop(0, x_ref.shape[0] // block, rows, 0)


def base_kernel(half_ref, w_ref, x_ref, o_ref, rest_ref, sem):
    rows = rest_ref.shape[0]
    copy = pltpu.make_async_copy(x_ref.at[pl.ds(rows, rows)], rest_ref, sem)
    copy.start()
    multiply(half_ref, w_ref, o_ref)
    copy.wait()


def base_first(half, w, x):
    rows, n = half.shape[0], w.shape[1]
    return pl.pallas_call(
        base_kernel,
        in_specs=[VMEM, VMEM, HBM],
        out_specs=[VMEM, VMEM],
        out_shape=[jax.ShapeDtypeStruct((rows, n), F32), jax.ShapeDtypeStruct(half.shape, BF)],
        scratch_shapes=[pltpu.SemaphoreType.DMA],
        compiler_params=params(28),
        cost_estimate=cost(1000000, 1 << 20),
        name="base_first",
    )(half, w, x)


def base_second(rest, w):
    return pl.pallas_call(
        multiply,
        in_specs=[VMEM, VMEM],
        out_specs=VMEM,
        out_shape=jax.ShapeDtypeStruct((rest.shape[0], w.shape[1]), F32),
        compiler_params=params(12),
        cost_estimate=cost(1000000, 1 << 20),
        name="base_second",
    )(rest, w)


def shrink_kernel(groups, has_sum, last, code_ref, x_ref, *refs):
    code = code_ref[...]
    refs = list(refs)
    total = None
    for count, places in groups:
        parts = [refs.pop(0)[...] for _ in range(count)]
        a = parts[0] if count == 1 else jnp.concatenate(parts, axis=0)
        p = lax.dot_general(x_ref[...], a, (((1,), (1,)), ((), ())), preferred_element_type=F32)
        for k, (j, i) in enumerate(places):
            term = jnp.where(code == owner(j, i), p[:, 128 * k : 128 * k + 128], 0.0)
            total = term if total is None else total + term
    if has_sum:
        total = total + refs.pop(0)[...]
    if not last:
        refs[0][...] = total
        return
    keep_ref, give_ref = refs
    half = total.shape[0] // 2
    folded = total + pltpu.roll(total, 64, 1)
    lane = lax.broadcasted_iota(jnp.int32, (half, 128), 1)
    packed = jnp.where(lane < 64, folded[:half], folded[half:])
    low, high = packed[: half // 2], packed[half // 2 :]
    core = lax.axis_index("tp") % 2
    keep_ref[...] = jnp.where(core == 0, low, high)
    give_ref[...] = jnp.where(core == 0, high, low)


def shrink(code, x, groups, total, last, name, weight=1 << 20):
    m = x.shape[0]
    args = [code, x] + [a for parts, _ in groups for a in parts] + ([] if total is None else [total])
    rows = m // 4 if last else m
    shape = jax.ShapeDtypeStruct((rows, 128), F32)
    return pl.pallas_call(
        functools.partial(
            shrink_kernel, [(len(parts), places) for parts, places in groups], total is not None, last
        ),
        in_specs=[VMEM] * len(args),
        out_specs=[VMEM] * 2 if last else VMEM,
        out_shape=[shape] * 2 if last else shape,
        compiler_params=params(16),
        cost_estimate=cost(weight, 1 << 20),
        name=name,
    )(*args)


def expand_kernel(groups, code_ref, mine_ref, other_ref, top_ref, bottom_ref, *refs):
    b_refs, o_ref = refs[:-1], refs[-1]
    block = o_ref.shape[0]
    step = pl.program_id(0)
    here = pl.ds(pl.multiple_of(step * block, block), block)
    code = code_ref[here, :]
    core = lax.axis_index("tp") % 2
    mine, other = mine_ref[...].astype(F32), other_ref[...].astype(F32)
    packed = jnp.concatenate(
        [jnp.where(core == 0, mine, other), jnp.where(core == 0, other, mine)], axis=0
    )
    lane = lax.broadcasted_iota(jnp.int32, packed.shape, 1)
    left = (lane < 64) == (step == 0)
    rows = jnp.where(left, packed, pltpu.roll(packed, 64, 1))
    delta = None
    for (places, ref_at, lanes), b_ref in zip(groups, b_refs):
        spread = jnp.concatenate(
            [jnp.where(code == owner(j, i), rows, 0.0).astype(BF) for j, i in places], axis=1
        )
        d = jnp.dot(spread, b_ref[ref_at:, lanes : lanes + o_ref.shape[1]], preferred_element_type=F32)
        delta = d if delta is None else delta + d
    delta = delta.astype(BF).astype(F32)
    for i, base_ref in enumerate((top_ref, bottom_ref)):

        @pl.when(step == i)
        def _(base_ref=base_ref):
            o_ref[...] = (base_ref[...] + adapter_scale * delta).astype(BF)


def expand(code, mine, other, base, parts):
    block, n = base[0].shape
    m = 2 * block
    args = [code, mine, other, *base] + [part[0] for part in parts]
    return pl.pallas_call(
        functools.partial(expand_kernel, [part[1:] for part in parts]),
        grid=(2,),
        in_specs=[VMEM] * len(args),
        out_specs=pl.BlockSpec((block, n), lambda i: (i, 0)),
        out_shape=jax.ShapeDtypeStruct((m, n), BF),
        compiler_params=params(12),
        cost_estimate=cost(2 * m * n * 2048, 6 * m * n),
        name="expand",
    )(*args)


def tie(*arrays):
    return lax.optimization_barrier(arrays)


def per_device(activations, token_adapter_index, query_matrix, down, up):
    down = jnp.swapaxes(down, 1, 2).reshape(128, -1)
    up = up.reshape(128, -1)
    width, columns = down.shape[1], up.shape[1]
    row = lambda j, hops=HOPS: [(j, i) for i in hops]

    before, after = first(down, 1), first(down, -1)
    code = mask_code(token_adapter_index)
    both, code = tie(jnp.concatenate([down, up], axis=1), code)
    far = first(both, 2)
    close = jnp.concatenate([both[:, :width], before, after], axis=0)
    a_before, a_after = second(close, 1), second(close, -1)
    here, half = fetch(tie(activations, before, after)[0], width)
    late_up = tie(up, code)[0]
    u_near = [first(late_up, d) for d in (1, -1)]

    far, half, *u_near = tie(far, half, *u_near)
    d_far = far[:, :width]
    u_own = [jnp.concatenate([up, u_near[0]], axis=0), jnp.concatenate([u_near[1], far[:, width:]], axis=0)]
    load = jnp.concatenate([d_far, jnp.concatenate(u_own, axis=1)], axis=0)
    b_before, b_after = second(load, 1), second(load, -1)
    top, rest = base_first(half, query_matrix, activations)
    base = [top, base_second(rest, query_matrix)]
    a_before, a_after, base[1] = tie(a_before, a_after, base[1])
    groups = [([close, d_far], row(0)), ([a_before], row(-1, HOPS[:3])), ([a_after], row(1, HOPS[:3]))]
    total = shrink(code, here, groups, None, False, "shrink_near", 20000000000)
    d_two = [second(a_before[:256], 1), second(jnp.concatenate([a_after[256:], b_after[:128]]), -1)]
    total, u_before, u_after = tie(total, b_before[128:, :columns], b_after[128:, columns:])
    u_two = [second(u_before, 1), second(u_after, -1)]
    groups = [([b_before[:128], b_after[:128]], [(-1, 2), (1, 2)])]
    total = shrink(code, here, groups, total, False, "shrink_side")
    *d_two, total = tie(*d_two, total)
    keep, give = shrink(code, here, [(d_two, row(2))], total, True, "shrink_far")
    keep, give, *u_two = tie(keep, give, *u_two)
    keep = keep + other_core(give)
    keep = keep + pair(keep, 0)
    keep = keep + pair(keep, 1)
    mine = keep.astype(BF)
    parts = []
    for j, a, at in ((0, load, 128), (-1, b_before, 128), (1, b_after, 128)):
        parts += [(a, row(j, HOPS[:2]), at, 0), (a, row(j, HOPS[2:]), at, columns)]
    parts += [(a, row(2, hops), 0, 0) for a, hops in zip(u_two, (HOPS[:2], HOPS[2:]))]
    return expand(code, mine, other_core(mine), base, parts)


def solution(mesh):
    in_specs = (
        P("rep", None),
        P("rep", None),
        P(None, "tp"),
        P("rep", "tp", None),
        P("rep", None, "tp"),
    )
    return jax.shard_map(
        per_device, mesh=mesh, in_specs=in_specs, out_specs=P("rep", "tp"), check_vma=False
    )
```

```python
import functools

import jax
import jax.numpy as jnp
from jax import lax
from jax.experimental import pallas as pl
from jax.experimental.pallas import tpu as pltpu
from jax.sharding import PartitionSpec as P

BF, F32 = jnp.bfloat16, jnp.float32
AXES = ("rep", "tp")
RING = 4
HOPS = (0, -1, 1, 2)
adapter_scale = 0.5


def device_of(x, y, z, c):
    return (z % RING * RING + x % RING) * 2 * RING + y % RING * 2 + c


def every(f):
    return [
        (device_of(x, y, z, c), device_of(*f(x, y, z, c)))
        for z in range(RING)
        for x in range(RING)
        for y in range(RING)
        for c in range(2)
    ]


def first(a, d):
    return lax.ppermute(
        a, AXES, every(lambda x, y, z, c: (x, y, z + d, c) if c else (x + d, y, z, c))
    )


def second(a, d):
    return lax.ppermute(
        a, AXES, every(lambda x, y, z, c: (x + d, y, z, c) if c else (x, y, z + d, c))
    )


def other_core(a):
    return lax.ppermute(a, AXES, every(lambda x, y, z, c: (x, y, z, 1 - c)))


def pair(a, step):
    def to(x, y, z, c):
        return (x, (y ^ 1) if (c + step) % 2 == 0 else (3 - y), z, c)

    return lax.ppermute(a, AXES, every(to))


def params(mib):
    return pltpu.CompilerParams(vmem_limit_bytes=mib << 20)


def cost(flops, moved):
    return pl.CostEstimate(flops=flops, bytes_accessed=moved, transcendentals=0)


VMEM = pl.BlockSpec(memory_space=pltpu.VMEM)
HBM = pl.BlockSpec(memory_space=pltpu.HBM)


def owner(j, i):
    rep, core = lax.axis_index("rep"), lax.axis_index("tp") % 2
    dz, dx = jnp.where(core == 0, j, i), jnp.where(core == 0, i, j)
    return (rep // RING + dz + RING) % RING * RING + (rep % RING + dx + RING) % RING


def code_kernel(ident_ref, code_ref):
    side = lax.broadcasted_iota(jnp.int32, (128, 128), 1) // 64
    for r in range(ident_ref.shape[0]):
        ident = jnp.broadcast_to(ident_ref[r : r + 1, :], (128, 128)).T
        code_ref[128 * r : 128 * r + 128, :] = jnp.where((ident & 1) == side, ident >> 1, -1)


def mask_code(ident):
    m = ident.shape[0]
    return pl.pallas_call(
        code_kernel,
        in_specs=[VMEM],
        out_specs=VMEM,
        out_shape=jax.ShapeDtypeStruct((m, 128), jnp.int32),
        compiler_params=params(2),
        cost_estimate=cost(1 << 20, 1 << 20),
        name="mask_code",
    )(ident.reshape(m // 128, 128))


def fetch_kernel(x_ref, here_ref, half_ref, sems):
    width, rows = here_ref.shape[1], half_ref.shape[0]
    at = pl.multiple_of(lax.axis_index("tp") * width, width)
    here = pltpu.make_async_copy(x_ref.at[:, pl.ds(at, width)], here_ref, sems.at[0])
    half = pltpu.make_async_copy(x_ref.at[pl.ds(0, rows)], half_ref, sems.at[1])
    here.start()
    half.start()
    here.wait()
    half.wait()


def fetch(x, width):
    m, k = x.shape
    return pl.pallas_call(
        fetch_kernel,
        in_specs=[HBM],
        out_specs=[VMEM] * 2,
        out_shape=[jax.ShapeDtypeStruct((m, width), BF), jax.ShapeDtypeStruct((m // 2, k), BF)],
        scratch_shapes=[pltpu.SemaphoreType.DMA((2,))],
        compiler_params=params(28),
        cost_estimate=cost(1000000, 1 << 20),
        name="fetch",
    )(x)


def multiply(x_ref, w_ref, o_ref, block=256):
    def rows(i, _):
        at = pl.ds(pl.multiple_of(i * block, block), block)
        o_ref[at, :] = jnp.dot(x_ref[at, :], w_ref[...], preferred_element_type=F32)
        return 0

    lax.fori_loop(0, x_ref.shape[0] // block, rows, 0)


def base_kernel(half_ref, w_ref, x_ref, o_ref, rest_ref, sem):
    rows = rest_ref.shape[0]
    copy = pltpu.make_async_copy(x_ref.at[pl.ds(rows, rows)], rest_ref, sem)
    copy.start()
    multiply(half_ref, w_ref, o_ref)
    copy.wait()


def base_first(half, w, x):
    rows, n = half.shape[0], w.shape[1]
    return pl.pallas_call(
        base_kernel,
        in_specs=[VMEM, VMEM, HBM],
        out_specs=[VMEM, VMEM],
        out_shape=[jax.ShapeDtypeStruct((rows, n), F32), jax.ShapeDtypeStruct(half.shape, BF)],
        scratch_shapes=[pltpu.SemaphoreType.DMA],
        compiler_params=params(28),
        cost_estimate=cost(5000000000, 1 << 20),
        name="base_first",
    )(half, w, x)


def base_second(rest, w):
    return pl.pallas_call(
        multiply,
        in_specs=[VMEM, VMEM],
        out_specs=VMEM,
        out_shape=jax.ShapeDtypeStruct((rest.shape[0], w.shape[1]), F32),
        compiler_params=params(12),
        cost_estimate=cost(5000000000, 1 << 20),
        name="base_second",
    )(rest, w)


def shrink_kernel(groups, has_sum, last, code_ref, x_ref, *refs):
    code = code_ref[...]
    refs = list(refs)
    total = None
    for count, places in groups:
        parts = [refs.pop(0)[...] for _ in range(count)]
        a = parts[0] if count == 1 else jnp.concatenate(parts, axis=0)
        p = lax.dot_general(x_ref[...], a, (((1,), (1,)), ((), ())), preferred_element_type=F32)
        for k, (j, i) in enumerate(places):
            term = jnp.where(code == owner(j, i), p[:, 128 * k : 128 * k + 128], 0.0)
            total = term if total is None else total + term
    if has_sum:
        total = total + refs.pop(0)[...]
    if not last:
        refs[0][...] = total
        return
    keep_ref, give_ref = refs
    half = total.shape[0] // 2
    folded = total + pltpu.roll(total, 64, 1)
    lane = lax.broadcasted_iota(jnp.int32, (half, 128), 1)
    packed = jnp.where(lane < 64, folded[:half], folded[half:])
    low, high = packed[: half // 2], packed[half // 2 :]
    core = lax.axis_index("tp") % 2
    keep_ref[...] = jnp.where(core == 0, low, high)
    give_ref[...] = jnp.where(core == 0, high, low)


def shrink(code, x, groups, total, last, name, weight=1 << 20):
    m = x.shape[0]
    args = [code, x] + [a for parts, _ in groups for a in parts] + ([] if total is None else [total])
    rows = m // 4 if last else m
    shape = jax.ShapeDtypeStruct((rows, 128), F32)
    return pl.pallas_call(
        functools.partial(
            shrink_kernel, [(len(parts), places) for parts, places in groups], total is not None, last
        ),
        in_specs=[VMEM] * len(args),
        out_specs=[VMEM] * 2 if last else VMEM,
        out_shape=[shape] * 2 if last else shape,
        compiler_params=params(16),
        cost_estimate=cost(weight, 1 << 20),
        name=name,
    )(*args)


def expand_kernel(groups, code_ref, mine_ref, other_ref, top_ref, bottom_ref, *refs):
    b_refs, o_ref = refs[:-1], refs[-1]
    block = o_ref.shape[0]
    step = pl.program_id(0)
    here = pl.ds(pl.multiple_of(step * block, block), block)
    code = code_ref[here, :]
    core = lax.axis_index("tp") % 2
    mine, other = mine_ref[...].astype(F32), other_ref[...].astype(F32)
    packed = jnp.concatenate(
        [jnp.where(core == 0, mine, other), jnp.where(core == 0, other, mine)], axis=0
    )
    lane = lax.broadcasted_iota(jnp.int32, packed.shape, 1)
    left = (lane < 64) == (step == 0)
    rows = jnp.where(left, packed, pltpu.roll(packed, 64, 1))
    delta = None
    for (places, ref_at, lanes), b_ref in zip(groups, b_refs):
        spread = jnp.concatenate(
            [jnp.where(code == owner(j, i), rows, 0.0).astype(BF) for j, i in places], axis=1
        )
        d = jnp.dot(spread, b_ref[ref_at:, lanes : lanes + o_ref.shape[1]], preferred_element_type=F32)
        delta = d if delta is None else delta + d
    delta = delta.astype(BF).astype(F32)
    for i, base_ref in enumerate((top_ref, bottom_ref)):

        @pl.when(step == i)
        def _(base_ref=base_ref):
            o_ref[...] = (base_ref[...] + adapter_scale * delta).astype(BF)


def expand(code, mine, other, base, parts):
    block, n = base[0].shape
    m = 2 * block
    args = [code, mine, other, *base] + [part[0] for part in parts]
    return pl.pallas_call(
        functools.partial(expand_kernel, [part[1:] for part in parts]),
        grid=(2,),
        in_specs=[VMEM] * len(args),
        out_specs=pl.BlockSpec((block, n), lambda i: (i, 0)),
        out_shape=jax.ShapeDtypeStruct((m, n), BF),
        compiler_params=params(12),
        cost_estimate=cost(2 * m * n * 2048, 6 * m * n),
        name="expand",
    )(*args)


def tie(*arrays):
    return lax.optimization_barrier(arrays)


def per_device(activations, token_adapter_index, query_matrix, down, up):
    down = jnp.swapaxes(down, 1, 2).reshape(128, -1)
    up = up.reshape(128, -1)
    width = down.shape[1]
    row = lambda j, hops=HOPS: [(j, i) for i in hops]

    near = [first(down, d) for d in (1, -1, 2)]
    code = mask_code(token_adapter_index)
    here, half = fetch(tie(activations, code)[0], width)
    near, here, half, up = tie(near, here, half, up)
    d_own = jnp.concatenate([down, *near], axis=0)
    d_before, d_after = second(d_own, 1), second(d_own, -1)
    u_own = jnp.concatenate([up] + [first(up, d) for d in (1, -1, 2)], axis=0)
    top, rest = base_first(half, query_matrix, activations)
    d_before, d_after, top = tie(d_before, d_after, top)

    d_two = [second(d_before[:256], 1), second(d_after[256:], -1)]
    groups = [([d_own], row(0)), ([d_before], row(-1)), ([d_after], row(1))]
    total = shrink(code, here, groups, None, False, "shrink_near", 5000000000)
    total, u_own = tie(total, u_own)
    u_before, u_after = second(u_own, 1), second(u_own, -1)
    *d_two, total = tie(*d_two, total)
    keep, give = shrink(code, here, [(d_two, row(2))], total, True, "shrink_far")
    keep = keep + other_core(give)
    u_two = [second(u_before[:256], 1), second(u_after[256:], -1)]
    keep = keep + pair(keep, 0)
    there, bottom, *u_two = tie(pair(keep, 1), base_second(rest, query_matrix), *u_two)
    keep = keep + there
    mine = keep.astype(BF)
    parts = [(u_own, row(0), 0, 0), (u_before, row(-1), 0, 0), (u_after, row(1), 0, 0)]
    parts += [(a, row(2, hops), 0, 0) for a, hops in zip(u_two, (HOPS[:2], HOPS[2:]))]
    return expand(code, mine, other_core(mine), [top, bottom], parts)


def solution(mesh):
    in_specs = (
        P("rep", None),
        P("rep", None),
        P(None, "tp"),
        P("rep", "tp", None),
        P("rep", None, "tp"),
    )
    return jax.shard_map(
        per_device, mesh=mesh, in_specs=in_specs, out_specs=P("rep", "tp"), check_vma=False
    )
```

```python
import functools

import jax
import jax.numpy as jnp
from jax import lax
from jax.experimental import pallas as pl
from jax.experimental.pallas import tpu as pltpu
from jax.sharding import PartitionSpec as P

BF, F32 = jnp.bfloat16, jnp.float32
AXES = ("rep", "tp")
RING = 4
HOPS = (0, -1, 1, 2)
adapter_scale = 0.5


def device_of(x, y, z, c):
    return (z % RING * RING + x % RING) * 2 * RING + y % RING * 2 + c


def every(f):
    return [
        (device_of(x, y, z, c), device_of(*f(x, y, z, c)))
        for z in range(RING)
        for x in range(RING)
        for y in range(RING)
        for c in range(2)
    ]


def first(a, d):
    return lax.ppermute(
        a, AXES, every(lambda x, y, z, c: (x, y, z + d, c) if c else (x + d, y, z, c))
    )


def second(a, d):
    return lax.ppermute(
        a, AXES, every(lambda x, y, z, c: (x + d, y, z, c) if c else (x, y, z + d, c))
    )


def other_core(a):
    return lax.ppermute(a, AXES, every(lambda x, y, z, c: (x, y, z, 1 - c)))


def pair(a, step):
    def to(x, y, z, c):
        return (x, (y ^ 1) if (c + step) % 2 == 0 else (3 - y), z, c)

    return lax.ppermute(a, AXES, every(to))


def params(mib):
    return pltpu.CompilerParams(vmem_limit_bytes=mib << 20)


def cost(flops, moved):
    return pl.CostEstimate(flops=flops, bytes_accessed=moved, transcendentals=0)


VMEM = pl.BlockSpec(memory_space=pltpu.VMEM)
HBM = pl.BlockSpec(memory_space=pltpu.HBM)


def owner(j, i):
    rep, core = lax.axis_index("rep"), lax.axis_index("tp") % 2
    dz, dx = jnp.where(core == 0, j, i), jnp.where(core == 0, i, j)
    return (rep // RING + dz + RING) % RING * RING + (rep % RING + dx + RING) % RING


def code_kernel(ident_ref, code_ref):
    side = lax.broadcasted_iota(jnp.int32, (128, 128), 1) // 64
    for r in range(ident_ref.shape[0]):
        ident = jnp.broadcast_to(ident_ref[r : r + 1, :], (128, 128)).T
        code_ref[128 * r : 128 * r + 128, :] = jnp.where((ident & 1) == side, ident >> 1, -1)


def mask_code(ident):
    m = ident.shape[0]
    return pl.pallas_call(
        code_kernel,
        in_specs=[VMEM],
        out_specs=VMEM,
        out_shape=jax.ShapeDtypeStruct((m, 128), jnp.int32),
        compiler_params=params(2),
        cost_estimate=cost(1 << 20, 1 << 20),
        name="mask_code",
    )(ident.reshape(m // 128, 128))


def fetch_kernel(x_ref, here_ref, half_ref, sems):
    width, rows = here_ref.shape[1], half_ref.shape[0]
    at = pl.multiple_of(lax.axis_index("tp") * width, width)
    here = pltpu.make_async_copy(x_ref.at[:, pl.ds(at, width)], here_ref, sems.at[0])
    half = pltpu.make_async_copy(x_ref.at[pl.ds(0, rows)], half_ref, sems.at[1])
    here.start()
    half.start()
    here.wait()
    half.wait()


def fetch(x, width):
    m, k = x.shape
    return pl.pallas_call(
        fetch_kernel,
        in_specs=[HBM],
        out_specs=[VMEM] * 2,
        out_shape=[jax.ShapeDtypeStruct((m, width), BF), jax.ShapeDtypeStruct((m // 2, k), BF)],
        scratch_shapes=[pltpu.SemaphoreType.DMA((2,))],
        compiler_params=params(28),
        cost_estimate=cost(1000000, 1 << 20),
        name="fetch",
    )(x)


def multiply(x_ref, w_ref, o_ref, rows, at=0, block=256):
    def step(i, _):
        here = pl.ds(pl.multiple_of(i * block, block), block)
        there = pl.ds(pl.multiple_of(at + i * block, block), block)
        o_ref[there, :] = jnp.dot(x_ref[here, :], w_ref[...], preferred_element_type=F32)
        return 0

    lax.fori_loop(0, rows // block, step, 0)


def base_kernel(half_ref, w_ref, x_ref, o_ref, rest_ref, xb, sems):
    half, most, last = half_ref.shape[0], o_ref.shape[0], rest_ref.shape[0]
    copies = [
        pltpu.make_async_copy(x_ref.at[pl.ds(half, most - half)], xb, sems.at[0]),
        pltpu.make_async_copy(x_ref.at[pl.ds(most, last)], rest_ref, sems.at[1]),
    ]
    for copy in copies:
        copy.start()
    multiply(half_ref, w_ref, o_ref, half)
    copies[0].wait()
    multiply(xb, w_ref, o_ref, most - half, half)
    copies[1].wait()


def base_first(half, w, x):
    (m, k), n = x.shape, w.shape[1]
    return pl.pallas_call(
        base_kernel,
        in_specs=[VMEM, VMEM, HBM],
        out_specs=[VMEM, VMEM],
        out_shape=[jax.ShapeDtypeStruct((m * 3 // 4, n), F32), jax.ShapeDtypeStruct((m // 4, k), BF)],
        scratch_shapes=[pltpu.VMEM((m // 4, k), BF), pltpu.SemaphoreType.DMA((2,))],
        compiler_params=params(28),
        cost_estimate=cost(5000000000, 1 << 20),
        name="base_first",
    )(half, w, x)


def base_second_kernel(x_ref, w_ref, o_ref):
    multiply(x_ref, w_ref, o_ref, x_ref.shape[0])


def base_second(rest, w):
    return pl.pallas_call(
        base_second_kernel,
        in_specs=[VMEM, VMEM],
        out_specs=VMEM,
        out_shape=jax.ShapeDtypeStruct((rest.shape[0], w.shape[1]), F32),
        compiler_params=params(12),
        cost_estimate=cost(5000000000, 1 << 20),
        name="base_second",
    )(rest, w)


def shrink_kernel(groups, has_sum, last, code_ref, x_ref, *refs):
    code = code_ref[...]
    refs = list(refs)
    total = None
    for count, places in groups:
        parts = [refs.pop(0)[...] for _ in range(count)]
        a = parts[0] if count == 1 else jnp.concatenate(parts, axis=0)
        p = lax.dot_general(x_ref[...], a, (((1,), (1,)), ((), ())), preferred_element_type=F32)
        for k, (j, i) in enumerate(places):
            term = jnp.where(code == owner(j, i), p[:, 128 * k : 128 * k + 128], 0.0)
            total = term if total is None else total + term
    if has_sum:
        total = total + refs.pop(0)[...]
    if not last:
        refs[0][...] = total
        return
    keep_ref, give_ref = refs
    half = total.shape[0] // 2
    folded = total + pltpu.roll(total, 64, 1)
    lane = lax.broadcasted_iota(jnp.int32, (half, 128), 1)
    packed = jnp.where(lane < 64, folded[:half], folded[half:])
    low, high = packed[: half // 2], packed[half // 2 :]
    core = lax.axis_index("tp") % 2
    keep_ref[...] = jnp.where(core == 0, low, high)
    give_ref[...] = jnp.where(core == 0, high, low)


def shrink(code, x, groups, total, last, name, weight=1 << 20):
    m = x.shape[0]
    args = [code, x] + [a for parts, _ in groups for a in parts] + ([] if total is None else [total])
    rows = m // 4 if last else m
    shape = jax.ShapeDtypeStruct((rows, 128), F32)
    return pl.pallas_call(
        functools.partial(
            shrink_kernel, [(len(parts), places) for parts, places in groups], total is not None, last
        ),
        in_specs=[VMEM] * len(args),
        out_specs=[VMEM] * 2 if last else VMEM,
        out_shape=[shape] * 2 if last else shape,
        compiler_params=params(16),
        cost_estimate=cost(weight, 1 << 20),
        name=name,
    )(*args)


def expand_kernel(groups, code_ref, mine_ref, other_ref, top_ref, bottom_ref, *refs):
    b_refs, o_ref = refs[:-1], refs[-1]
    block = o_ref.shape[0]
    step = pl.program_id(0)
    here = pl.ds(pl.multiple_of(step * block, block), block)
    code = code_ref[here, :]
    core = lax.axis_index("tp") % 2
    mine, other = mine_ref[...].astype(F32), other_ref[...].astype(F32)
    packed = jnp.concatenate(
        [jnp.where(core == 0, mine, other), jnp.where(core == 0, other, mine)], axis=0
    )
    lane = lax.broadcasted_iota(jnp.int32, packed.shape, 1)
    left = (lane < 64) == (step == 0)
    rows = jnp.where(left, packed, pltpu.roll(packed, 64, 1))
    delta = None
    for (places, ref_at, lanes), b_ref in zip(groups, b_refs):
        spread = jnp.concatenate(
            [jnp.where(code == owner(j, i), rows, 0.0).astype(BF) for j, i in places], axis=1
        )
        d = jnp.dot(spread, b_ref[ref_at:, lanes : lanes + o_ref.shape[1]], preferred_element_type=F32)
        delta = d if delta is None else delta + d
    delta = delta.astype(BF).astype(F32)
    quarter = block // 2

    @pl.when(step == 0)
    def _():
        o_ref[...] = (top_ref[:block, :] + adapter_scale * delta).astype(BF)

    @pl.when(step == 1)
    def _():
        o_ref[:quarter, :] = (top_ref[block:, :] + adapter_scale * delta[:quarter]).astype(BF)
        o_ref[quarter:, :] = (bottom_ref[...] + adapter_scale * delta[quarter:]).astype(BF)


def expand(code, mine, other, base, parts):
    m, n = code.shape[0], base[0].shape[1]
    block = m // 2
    args = [code, mine, other, *base] + [part[0] for part in parts]
    return pl.pallas_call(
        functools.partial(expand_kernel, [part[1:] for part in parts]),
        grid=(2,),
        in_specs=[VMEM] * len(args),
        out_specs=pl.BlockSpec((block, n), lambda i: (i, 0)),
        out_shape=jax.ShapeDtypeStruct((m, n), BF),
        compiler_params=params(12),
        cost_estimate=cost(2 * m * n * 2048, 6 * m * n),
        name="expand",
    )(*args)


def tie(*arrays):
    return lax.optimization_barrier(arrays)


def per_device(activations, token_adapter_index, query_matrix, down, up):
    down = jnp.swapaxes(down, 1, 2).reshape(128, -1)
    up = up.reshape(128, -1)
    width = down.shape[1]
    row = lambda j, hops=HOPS: [(j, i) for i in hops]

    near = [first(down, d) for d in (1, -1, 2)]
    code = mask_code(token_adapter_index)
    here, half = fetch(tie(activations, code)[0], width)
    near, here, half, up = tie(near, here, half, up)
    d_own = jnp.concatenate([down, *near], axis=0)
    d_before, d_after = second(d_own, 1), second(d_own, -1)
    u_own = jnp.concatenate([up] + [first(up, d) for d in (1, -1, 2)], axis=0)
    top, rest = base_first(half, query_matrix, activations)
    d_before, d_after, top = tie(d_before, d_after, top)

    d_two = [second(d_before[:256], 1), second(d_after[256:], -1)]
    groups = [([d_own], row(0)), ([d_before], row(-1)), ([d_after], row(1))]
    total = shrink(code, here, groups, None, False, "shrink_near", 5000000000)
    total, u_own = tie(total, u_own)
    u_before, u_after = second(u_own, 1), second(u_own, -1)
    *d_two, total = tie(*d_two, total)
    keep, give = shrink(code, here, [(d_two, row(2))], total, True, "shrink_far")
    keep = keep + other_core(give)
    u_two = [second(u_before[:256], 1), second(u_after[256:], -1)]
    keep = keep + pair(keep, 0)
    there, bottom, *u_two = tie(pair(keep, 1), base_second(rest, query_matrix), *u_two)
    keep = keep + there
    mine = keep.astype(BF)
    parts = [(u_own, row(0), 0, 0), (u_before, row(-1), 0, 0), (u_after, row(1), 0, 0)]
    parts += [(a, row(2, hops), 0, 0) for a, hops in zip(u_two, (HOPS[:2], HOPS[2:]))]
    return expand(code, mine, other_core(mine), [top, bottom], parts)


def solution(mesh):
    in_specs = (
        P("rep", None),
        P("rep", None),
        P(None, "tp"),
        P("rep", "tp", None),
        P("rep", None, "tp"),
    )
    return jax.shard_map(
        per_device, mesh=mesh, in_specs=in_specs, out_specs=P("rep", "tp"), check_vma=False
    )
```

```python
import functools

import jax
import jax.numpy as jnp
from jax import lax
from jax.experimental import pallas as pl
from jax.experimental.pallas import tpu as pltpu
from jax.sharding import PartitionSpec as P

BF, F32 = jnp.bfloat16, jnp.float32
AXES = ("rep", "tp")
RING = 4
HOPS = (0, -1, 1, 2)
adapter_scale = 0.5


def device_of(x, y, z, c):
    return (z % RING * RING + x % RING) * 2 * RING + y % RING * 2 + c


def every(f):
    return [
        (device_of(x, y, z, c), device_of(*f(x, y, z, c)))
        for z in range(RING)
        for x in range(RING)
        for y in range(RING)
        for c in range(2)
    ]


def first(a, d):
    return lax.ppermute(
        a, AXES, every(lambda x, y, z, c: (x, y, z + d, c) if c else (x + d, y, z, c))
    )


def second(a, d):
    return lax.ppermute(
        a, AXES, every(lambda x, y, z, c: (x + d, y, z, c) if c else (x, y, z + d, c))
    )


def other_core(a):
    return lax.ppermute(a, AXES, every(lambda x, y, z, c: (x, y, z, 1 - c)))


def pair(a, step):
    def to(x, y, z, c):
        return (x, (y ^ 1) if (c + step) % 2 == 0 else (3 - y), z, c)

    return lax.ppermute(a, AXES, every(to))


def params(mib):
    return pltpu.CompilerParams(vmem_limit_bytes=mib << 20)


def cost(flops, moved):
    return pl.CostEstimate(flops=flops, bytes_accessed=moved, transcendentals=0)


VMEM = pl.BlockSpec(memory_space=pltpu.VMEM)
HBM = pl.BlockSpec(memory_space=pltpu.HBM)


def owner(j, i):
    rep, core = lax.axis_index("rep"), lax.axis_index("tp") % 2
    dz, dx = jnp.where(core == 0, j, i), jnp.where(core == 0, i, j)
    return (rep // RING + dz + RING) % RING * RING + (rep % RING + dx + RING) % RING


def code_kernel(ident_ref, code_ref):
    side = lax.broadcasted_iota(jnp.int32, (128, 128), 1) // 64
    for r in range(ident_ref.shape[0]):
        ident = jnp.broadcast_to(ident_ref[r : r + 1, :], (128, 128)).T
        code_ref[128 * r : 128 * r + 128, :] = jnp.where((ident & 1) == side, ident >> 1, -1)


def mask_code(ident):
    m = ident.shape[0]
    return pl.pallas_call(
        code_kernel,
        in_specs=[VMEM],
        out_specs=VMEM,
        out_shape=jax.ShapeDtypeStruct((m, 128), jnp.int32),
        compiler_params=params(2),
        cost_estimate=cost(1 << 20, 1 << 20),
        name="mask_code",
    )(ident.reshape(m // 128, 128))


def fetch_kernel(x_ref, here_ref, half_ref, sems):
    width, rows = here_ref.shape[1], half_ref.shape[0]
    at = pl.multiple_of(lax.axis_index("tp") * width, width)
    here = pltpu.make_async_copy(x_ref.at[:, pl.ds(at, width)], here_ref, sems.at[0])
    half = pltpu.make_async_copy(x_ref.at[pl.ds(0, rows)], half_ref, sems.at[1])
    here.start()
    half.start()
    here.wait()
    half.wait()


def fetch(x, width):
    m, k = x.shape
    return pl.pallas_call(
        fetch_kernel,
        in_specs=[HBM],
        out_specs=[VMEM] * 2,
        out_shape=[jax.ShapeDtypeStruct((m, width), BF), jax.ShapeDtypeStruct((m // 2, k), BF)],
        scratch_shapes=[pltpu.SemaphoreType.DMA((2,))],
        compiler_params=params(28),
        cost_estimate=cost(1000000, 1 << 20),
        name="fetch",
    )(x)


def multiply(x_ref, w_ref, o_ref, rows, at=0, block=256):
    def step(i, _):
        here = pl.ds(pl.multiple_of(i * block, block), block)
        there = pl.ds(pl.multiple_of(at + i * block, block), block)
        o_ref[there, :] = jnp.dot(x_ref[here, :], w_ref[...], preferred_element_type=F32)
        return 0

    lax.fori_loop(0, rows // block, step, 0)


def base_kernel(half_ref, w_ref, x_ref, o_ref, rest_ref, xb, sems):
    half, most, last = half_ref.shape[0], o_ref.shape[0], rest_ref.shape[0]
    copies = [
        pltpu.make_async_copy(x_ref.at[pl.ds(half, most - half)], xb, sems.at[0]),
        pltpu.make_async_copy(x_ref.at[pl.ds(most, last)], rest_ref, sems.at[1]),
    ]
    for copy in copies:
        copy.start()
    multiply(half_ref, w_ref, o_ref, half)
    copies[0].wait()
    multiply(xb, w_ref, o_ref, most - half, half)
    copies[1].wait()


def base_first(half, w, x):
    (m, k), n = x.shape, w.shape[1]
    return pl.pallas_call(
        base_kernel,
        in_specs=[VMEM, VMEM, HBM],
        out_specs=[VMEM, VMEM],
        out_shape=[jax.ShapeDtypeStruct((m * 3 // 4, n), F32), jax.ShapeDtypeStruct((m // 4, k), BF)],
        scratch_shapes=[pltpu.VMEM((m // 4, k), BF), pltpu.SemaphoreType.DMA((2,))],
        compiler_params=params(28),
        cost_estimate=cost(5000000000, 1 << 20),
        name="base_first",
    )(half, w, x)


def base_second_kernel(x_ref, w_ref, o_ref):
    multiply(x_ref, w_ref, o_ref, x_ref.shape[0])


def base_second(rest, w):
    return pl.pallas_call(
        base_second_kernel,
        in_specs=[VMEM, VMEM],
        out_specs=VMEM,
        out_shape=jax.ShapeDtypeStruct((rest.shape[0], w.shape[1]), F32),
        compiler_params=params(12),
        cost_estimate=cost(5000000000, 1 << 20),
        name="base_second",
    )(rest, w)


def shrink_kernel(groups, has_sum, last, code_ref, x_ref, *refs):
    code = code_ref[...]
    refs = list(refs)
    total = None
    for count, places in groups:
        parts = [refs.pop(0)[...] for _ in range(count)]
        a = parts[0] if count == 1 else jnp.concatenate(parts, axis=0)
        p = lax.dot_general(x_ref[...], a, (((1,), (1,)), ((), ())), preferred_element_type=F32)
        for k, (j, i) in enumerate(places):
            term = jnp.where(code == owner(j, i), p[:, 128 * k : 128 * k + 128], 0.0)
            total = term if total is None else total + term
    if has_sum:
        total = total + refs.pop(0)[...]
    if not last:
        refs[0][...] = total
        return
    keep_ref, give_ref = refs
    half = total.shape[0] // 2
    folded = total + pltpu.roll(total, 64, 1)
    lane = lax.broadcasted_iota(jnp.int32, (half, 128), 1)
    packed = jnp.where(lane < 64, folded[:half], folded[half:])
    low, high = packed[: half // 2], packed[half // 2 :]
    core = lax.axis_index("tp") % 2
    keep_ref[...] = jnp.where(core == 0, low, high)
    give_ref[...] = jnp.where(core == 0, high, low)


def shrink(code, x, groups, total, last, name, weight=1 << 20):
    m = x.shape[0]
    args = [code, x] + [a for parts, _ in groups for a in parts] + ([] if total is None else [total])
    rows = m // 4 if last else m
    shape = jax.ShapeDtypeStruct((rows, 128), F32)
    return pl.pallas_call(
        functools.partial(
            shrink_kernel, [(len(parts), places) for parts, places in groups], total is not None, last
        ),
        in_specs=[VMEM] * len(args),
        out_specs=[VMEM] * 2 if last else VMEM,
        out_shape=[shape] * 2 if last else shape,
        compiler_params=params(16),
        cost_estimate=cost(weight, 1 << 20),
        name=name,
    )(*args)


def expand_kernel(code_ref, mine_ref, other_ref, top_ref, bottom_ref, *refs):
    *b_refs, o_ref, b_all = refs
    block = o_ref.shape[0]
    step = pl.program_id(0)
    here = pl.ds(pl.multiple_of(step * block, block), block)
    code = code_ref[here, :]
    core = lax.axis_index("tp") % 2
    mine, other = mine_ref[...].astype(F32), other_ref[...].astype(F32)
    packed = jnp.concatenate(
        [jnp.where(core == 0, mine, other), jnp.where(core == 0, other, mine)], axis=0
    )
    lane = lax.broadcasted_iota(jnp.int32, packed.shape, 1)
    left = (lane < 64) == (step == 0)
    rows = jnp.where(left, packed, pltpu.roll(packed, 64, 1))
    n = o_ref.shape[1]

    @pl.when(step == 0)
    def _():
        for k in range(16):
            part, at = b_refs[k // 4], 64 * (k % 4)
            for side in range(2):
                b_all[pl.ds(128 * k + 64 * side, 64), :] = part[pl.ds(at, 64), n * side : n * side + n]

    spread = jnp.concatenate(
        [jnp.where(code == owner(j, i), rows, 0.0).astype(BF) for i in HOPS for j in HOPS], axis=1
    )
    delta = jnp.dot(spread, b_all[...], preferred_element_type=F32)
    delta = delta.astype(BF).astype(F32)
    quarter = block // 2

    @pl.when(step == 0)
    def _():
        o_ref[...] = (top_ref[:block, :] + adapter_scale * delta).astype(BF)

    @pl.when(step == 1)
    def _():
        o_ref[:quarter, :] = (top_ref[block:, :] + adapter_scale * delta[:quarter]).astype(BF)
        o_ref[quarter:, :] = (bottom_ref[...] + adapter_scale * delta[quarter:]).astype(BF)


def expand(code, mine, other, base, ups):
    m, n = code.shape[0], base[0].shape[1]
    block = m // 2
    args = [code, mine, other, *base, *ups]
    return pl.pallas_call(
        expand_kernel,
        grid=(2,),
        in_specs=[VMEM] * len(args),
        out_specs=pl.BlockSpec((block, n), lambda i: (i, 0)),
        out_shape=jax.ShapeDtypeStruct((m, n), BF),
        scratch_shapes=[pltpu.VMEM((2048, n), BF)],
        compiler_params=params(14),
        cost_estimate=cost(2 * m * n * 2048, 6 * m * n),
        name="expand",
    )(*args)


def tie(*arrays):
    return lax.optimization_barrier(arrays)


def per_device(activations, token_adapter_index, query_matrix, down, up):
    down = jnp.swapaxes(down, 1, 2).reshape(128, -1)
    up = up.reshape(128, -1)
    width = down.shape[1]
    row = lambda j, hops=HOPS: [(j, i) for i in hops]

    near = [first(down, d) for d in (1, -1, 2)]
    code = mask_code(token_adapter_index)
    here, half = fetch(tie(activations, code)[0], width)
    before, after, far, here, half = tie(*near, here, half)
    own_up = jnp.concatenate([up[:64], up[64:]], axis=1)
    top = jnp.concatenate([down, before, own_up], axis=0)
    bottom = jnp.concatenate([after, far, own_up], axis=0)
    top_before, bottom_after = second(top, 1), second(bottom, -1)
    bottom_before, top_after = second(bottom[:256], 1), second(top[:256], -1)
    base, rest = base_first(half, query_matrix, activations)
    top_before, bottom_after, base = tie(top_before, bottom_after, base)

    top_two, bottom_two = second(top_before, 1), second(bottom_after[:256], -1)
    groups = [
        ([top[:256], bottom[:256]], row(0)),
        ([top_before[:256], bottom_before], row(-1)),
        ([top_after, bottom_after[:256]], row(1)),
    ]
    total = shrink(code, here, groups, None, False, "shrink_near", 5000000000)
    top_two, bottom_two, total = tie(top_two, bottom_two, total)
    d_two = [top_two[:256], bottom_two]
    keep, give = shrink(code, here, [(d_two, row(2))], total, True, "shrink_far")
    keep = keep + other_core(give)
    column = jnp.concatenate([own_up] + [a[256:] for a in (top_before, bottom_after, top_two)], axis=0)
    ups = [column] + [first(column, d) for d in (1, -1, 2)]
    keep = keep + pair(keep, 0)
    there, last = tie(pair(keep, 1), base_second(rest, query_matrix))
    mine, *ups = tie((keep + there).astype(BF), *ups)
    return expand(code, mine, other_core(mine), [base, last], ups)


def solution(mesh):
    in_specs = (
        P("rep", None),
        P("rep", None),
        P(None, "tp"),
        P("rep", "tp", None),
        P("rep", None, "tp"),
    )
    return jax.shard_map(
        per_device, mesh=mesh, in_specs=in_specs, out_specs=P("rep", "tp"), check_vma=False
    )
```

```python
import functools

import jax
import jax.numpy as jnp
from jax import lax
from jax.experimental import pallas as pl
from jax.experimental.pallas import tpu as pltpu
from jax.sharding import PartitionSpec as P

BF, F32 = jnp.bfloat16, jnp.float32
AXES = ("rep", "tp")
RING = 4
HOPS = (0, -1, 1, 2)
adapter_scale = 0.5


def device_of(x, y, z, c):
    return (z % RING * RING + x % RING) * 2 * RING + y % RING * 2 + c


def every(f):
    return [
        (device_of(x, y, z, c), device_of(*f(x, y, z, c)))
        for z in range(RING)
        for x in range(RING)
        for y in range(RING)
        for c in range(2)
    ]


def first(a, d):
    return lax.ppermute(
        a, AXES, every(lambda x, y, z, c: (x, y, z + d, c) if c else (x + d, y, z, c))
    )


def second(a, d):
    return lax.ppermute(
        a, AXES, every(lambda x, y, z, c: (x + d, y, z, c) if c else (x, y, z + d, c))
    )


def other_core(a):
    return lax.ppermute(a, AXES, every(lambda x, y, z, c: (x, y, z, 1 - c)))


def pair(a, step):
    def to(x, y, z, c):
        return (x, (y ^ 1) if (c + step) % 2 == 0 else (3 - y), z, c)

    return lax.ppermute(a, AXES, every(to))


def params(mib):
    return pltpu.CompilerParams(vmem_limit_bytes=mib << 20)


def cost(flops, moved):
    return pl.CostEstimate(flops=flops, bytes_accessed=moved, transcendentals=0)


VMEM = pl.BlockSpec(memory_space=pltpu.VMEM)
HBM = pl.BlockSpec(memory_space=pltpu.HBM)


def owner(j, i):
    rep, core = lax.axis_index("rep"), lax.axis_index("tp") % 2
    dz, dx = jnp.where(core == 0, j, i), jnp.where(core == 0, i, j)
    return (rep // RING + dz + RING) % RING * RING + (rep % RING + dx + RING) % RING


def code_kernel(ident_ref, code_ref):
    side = lax.broadcasted_iota(jnp.int32, (128, 128), 1) // 64
    for r in range(ident_ref.shape[0]):
        ident = jnp.broadcast_to(ident_ref[r : r + 1, :], (128, 128)).T
        code_ref[128 * r : 128 * r + 128, :] = jnp.where((ident & 1) == side, ident >> 1, -1)


def mask_code(ident):
    m = ident.shape[0]
    return pl.pallas_call(
        code_kernel,
        in_specs=[VMEM],
        out_specs=VMEM,
        out_shape=jax.ShapeDtypeStruct((m, 128), jnp.int32),
        compiler_params=params(2),
        cost_estimate=cost(1 << 20, 1 << 20),
        name="mask_code",
    )(ident.reshape(m // 128, 128))


def fetch_kernel(x_ref, here_ref, half_ref, sems):
    width, rows = here_ref.shape[1], half_ref.shape[0]
    at = pl.multiple_of(lax.axis_index("tp") * width, width)
    here = pltpu.make_async_copy(x_ref.at[:, pl.ds(at, width)], here_ref, sems.at[0])
    half = pltpu.make_async_copy(x_ref.at[pl.ds(0, rows)], half_ref, sems.at[1])
    here.start()
    half.start()
    here.wait()
    half.wait()


def fetch(x, width):
    m, k = x.shape
    return pl.pallas_call(
        fetch_kernel,
        in_specs=[HBM],
        out_specs=[VMEM] * 2,
        out_shape=[jax.ShapeDtypeStruct((m, width), BF), jax.ShapeDtypeStruct((m // 2, k), BF)],
        scratch_shapes=[pltpu.SemaphoreType.DMA((2,))],
        compiler_params=params(28),
        cost_estimate=cost(1000000, 1 << 20),
        name="fetch",
    )(x)


def multiply(x_ref, w_ref, o_ref, rows, at=0, block=256):
    def step(i, _):
        here = pl.ds(pl.multiple_of(i * block, block), block)
        there = pl.ds(pl.multiple_of(at + i * block, block), block)
        o_ref[there, :] = jnp.dot(x_ref[here, :], w_ref[...], preferred_element_type=F32)
        return 0

    lax.fori_loop(0, rows // block, step, 0)


def base_kernel(half_ref, w_ref, x_ref, o_ref, rest_ref, xb, sems):
    half, most, last = half_ref.shape[0], o_ref.shape[0], rest_ref.shape[0]
    copies = [
        pltpu.make_async_copy(x_ref.at[pl.ds(half, most - half)], xb, sems.at[0]),
        pltpu.make_async_copy(x_ref.at[pl.ds(most, last)], rest_ref, sems.at[1]),
    ]
    for copy in copies:
        copy.start()
    multiply(half_ref, w_ref, o_ref, half)
    copies[0].wait()
    multiply(xb, w_ref, o_ref, most - half, half)
    copies[1].wait()


def base_first(half, w, x):
    (m, k), n = x.shape, w.shape[1]
    return pl.pallas_call(
        base_kernel,
        in_specs=[VMEM, VMEM, HBM],
        out_specs=[VMEM, VMEM],
        out_shape=[jax.ShapeDtypeStruct((m * 3 // 4, n), F32), jax.ShapeDtypeStruct((m // 4, k), BF)],
        scratch_shapes=[pltpu.VMEM((m // 4, k), BF), pltpu.SemaphoreType.DMA((2,))],
        compiler_params=params(28),
        cost_estimate=cost(5000000000, 1 << 20),
        name="base_first",
    )(half, w, x)


def base_second_kernel(x_ref, w_ref, o_ref):
    multiply(x_ref, w_ref, o_ref, x_ref.shape[0])


def base_second(rest, w):
    return pl.pallas_call(
        base_second_kernel,
        in_specs=[VMEM, VMEM],
        out_specs=VMEM,
        out_shape=jax.ShapeDtypeStruct((rest.shape[0], w.shape[1]), F32),
        compiler_params=params(12),
        cost_estimate=cost(5000000000, 1 << 20),
        name="base_second",
    )(rest, w)


def shrink_kernel(groups, has_sum, last, code_ref, x_ref, *refs):
    code = code_ref[...]
    refs = list(refs)
    total = None
    for count, places in groups:
        parts = [refs.pop(0)[...] for _ in range(count)]
        a = parts[0] if count == 1 else jnp.concatenate(parts, axis=0)
        p = lax.dot_general(x_ref[...], a, (((1,), (1,)), ((), ())), preferred_element_type=F32)
        for k, (j, i) in enumerate(places):
            term = jnp.where(code == owner(j, i), p[:, 128 * k : 128 * k + 128], 0.0)
            total = term if total is None else total + term
    if has_sum:
        total = total + refs.pop(0)[...]
    if not last:
        refs[0][...] = total
        return
    keep_ref, give_ref = refs
    half = total.shape[0] // 2
    folded = total + pltpu.roll(total, 64, 1)
    lane = lax.broadcasted_iota(jnp.int32, (half, 128), 1)
    packed = jnp.where(lane < 64, folded[:half], folded[half:])
    low, high = packed[: half // 2], packed[half // 2 :]
    core = lax.axis_index("tp") % 2
    keep_ref[...] = jnp.where(core == 0, low, high)
    give_ref[...] = jnp.where(core == 0, high, low)


def shrink(code, x, groups, total, last, name, weight=1 << 20):
    m = x.shape[0]
    args = [code, x] + [a for parts, _ in groups for a in parts] + ([] if total is None else [total])
    rows = m // 4 if last else m
    shape = jax.ShapeDtypeStruct((rows, 128), F32)
    return pl.pallas_call(
        functools.partial(
            shrink_kernel, [(len(parts), places) for parts, places in groups], total is not None, last
        ),
        in_specs=[VMEM] * len(args),
        out_specs=[VMEM] * 2 if last else VMEM,
        out_shape=[shape] * 2 if last else shape,
        compiler_params=params(16),
        cost_estimate=cost(weight, 1 << 20),
        name=name,
    )(*args)


def expand_kernel(code_ref, mine_ref, other_ref, top_ref, bottom_ref, *refs):
    *b_refs, o_ref, b_all = refs
    block = o_ref.shape[0]
    step = pl.program_id(0)
    here = pl.ds(pl.multiple_of(step * block, block), block)
    code = code_ref[here, :]
    core = lax.axis_index("tp") % 2
    mine, other = mine_ref[...].astype(F32), other_ref[...].astype(F32)
    packed = jnp.concatenate(
        [jnp.where(core == 0, mine, other), jnp.where(core == 0, other, mine)], axis=0
    )
    lane = lax.broadcasted_iota(jnp.int32, packed.shape, 1)
    left = (lane < 64) == (step == 0)
    rows = jnp.where(left, packed, pltpu.roll(packed, 64, 1))
    n = o_ref.shape[1]

    @pl.when(step == 0)
    def _():
        for k in range(16):
            i, j = k // 4, k % 4
            part, at = (b_refs[i], 64 * j) if j < 3 else (b_refs[4 + i // 2], 64 * (i % 2))
            for side in range(2):
                b_all[pl.ds(128 * k + 64 * side, 64), :] = part[pl.ds(at, 64), n * side : n * side + n]

    spread = jnp.concatenate(
        [jnp.where(code == owner(j, i), rows, 0.0).astype(BF) for i in HOPS for j in HOPS], axis=1
    )
    delta = jnp.dot(spread, b_all[...], preferred_element_type=F32)
    delta = delta.astype(BF).astype(F32)
    quarter = block // 2

    @pl.when(step == 0)
    def _():
        o_ref[...] = (top_ref[:block, :] + adapter_scale * delta).astype(BF)

    @pl.when(step == 1)
    def _():
        o_ref[:quarter, :] = (top_ref[block:, :] + adapter_scale * delta[:quarter]).astype(BF)
        o_ref[quarter:, :] = (bottom_ref[...] + adapter_scale * delta[quarter:]).astype(BF)


def expand(code, mine, other, base, ups):
    m, n = code.shape[0], base[0].shape[1]
    block = m // 2
    args = [code, mine, other, *base, *ups]
    return pl.pallas_call(
        expand_kernel,
        grid=(2,),
        in_specs=[VMEM] * len(args),
        out_specs=pl.BlockSpec((block, n), lambda i: (i, 0)),
        out_shape=jax.ShapeDtypeStruct((m, n), BF),
        scratch_shapes=[pltpu.VMEM((2048, n), BF)],
        compiler_params=params(14),
        cost_estimate=cost(2 * m * n * 2048, 6 * m * n),
        name="expand",
    )(*args)


def tie(*arrays):
    return lax.optimization_barrier(arrays)


def per_device(activations, token_adapter_index, query_matrix, down, up):
    down = jnp.swapaxes(down, 1, 2).reshape(128, -1)
    up = up.reshape(128, -1)
    width = down.shape[1]
    row = lambda j, hops=HOPS: [(j, i) for i in hops]

    near = [first(down, d) for d in (1, -1, 2)]
    code = mask_code(token_adapter_index)
    here, half = fetch(tie(activations, code)[0], width)
    before, after, far, here, half = tie(*near, here, half)
    own_up = jnp.concatenate([up[:64], up[64:]], axis=1)
    top = jnp.concatenate([down, before, own_up], axis=0)
    bottom = jnp.concatenate([after, far, own_up], axis=0)
    top_before, bottom_after = second(top, 1), second(bottom, -1)
    bottom_before, top_after = second(bottom[:256], 1), second(top[:256], -1)
    base, rest = base_first(half, query_matrix, activations)
    top_before, bottom_after, base = tie(top_before, bottom_after, base)

    d_two = [second(top_before[:256], 1), second(bottom_after[:256], -1)]
    groups = [
        ([top[:256], bottom[:256]], row(0)),
        ([top_before[:256], bottom_before], row(-1)),
        ([top_after, bottom_after[:256]], row(1)),
    ]
    total = shrink(code, here, groups, None, False, "shrink_near", 5000000000)
    column = jnp.concatenate([own_up, top_before[256:], bottom_after[256:]], axis=0)
    column, total = tie(column, total)
    ups = [first(column, d) for d in (1, -1, 2)]
    *d_two, total = tie(*d_two, total)
    keep, give = shrink(code, here, [(d_two, row(2))], total, True, "shrink_far")
    keep = keep + other_core(give)
    there, *ups = tie(pair(keep, 0), *ups)
    keep = keep + there
    ups = [column, *ups]
    up_two = [
        second(jnp.concatenate([a[64:128] for a in ups[:2]], axis=0), 1),
        second(jnp.concatenate([a[128:] for a in ups[2:]], axis=0), -1),
    ]
    there, last = tie(pair(keep, 1), base_second(rest, query_matrix))
    mine, *up_two = tie((keep + there).astype(BF), *up_two)
    return expand(code, mine, other_core(mine), [base, last], [*ups, *up_two])


def solution(mesh):
    in_specs = (
        P("rep", None),
        P("rep", None),
        P(None, "tp"),
        P("rep", "tp", None),
        P("rep", None, "tp"),
    )
    return jax.shard_map(
        per_device, mesh=mesh, in_specs=in_specs, out_specs=P("rep", "tp"), check_vma=False
    )
```

```python
import functools

import jax
import jax.numpy as jnp
from jax import lax
from jax.experimental import pallas as pl
from jax.experimental.pallas import tpu as pltpu
from jax.sharding import PartitionSpec as P

BF, F32 = jnp.bfloat16, jnp.float32
AXES = ("rep", "tp")
RING = 4
HOPS = (0, -1, 1, 2)
adapter_scale = 0.5


def device_of(x, y, z, c):
    return (z % RING * RING + x % RING) * 2 * RING + y % RING * 2 + c


def every(f):
    return [
        (device_of(x, y, z, c), device_of(*f(x, y, z, c)))
        for z in range(RING)
        for x in range(RING)
        for y in range(RING)
        for c in range(2)
    ]


def first(a, d):
    return lax.ppermute(
        a, AXES, every(lambda x, y, z, c: (x, y, z + d, c) if c else (x + d, y, z, c))
    )


def second(a, d):
    return lax.ppermute(
        a, AXES, every(lambda x, y, z, c: (x + d, y, z, c) if c else (x, y, z + d, c))
    )


def other_core(a):
    return lax.ppermute(a, AXES, every(lambda x, y, z, c: (x, y, z, 1 - c)))


def pair(a, step):
    def to(x, y, z, c):
        return (x, (y ^ 1) if (c + step) % 2 == 0 else (3 - y), z, c)

    return lax.ppermute(a, AXES, every(to))


def params(mib):
    return pltpu.CompilerParams(vmem_limit_bytes=mib << 20)


def cost(flops, moved):
    return pl.CostEstimate(flops=flops, bytes_accessed=moved, transcendentals=0)


VMEM = pl.BlockSpec(memory_space=pltpu.VMEM)
HBM = pl.BlockSpec(memory_space=pltpu.HBM)


def owner(j, i):
    rep, core = lax.axis_index("rep"), lax.axis_index("tp") % 2
    dz, dx = jnp.where(core == 0, j, i), jnp.where(core == 0, i, j)
    return (rep // RING + dz + RING) % RING * RING + (rep % RING + dx + RING) % RING


def code_kernel(ident_ref, code_ref):
    side = lax.broadcasted_iota(jnp.int32, (128, 128), 1) // 64
    for r in range(ident_ref.shape[0]):
        ident = jnp.broadcast_to(ident_ref[r : r + 1, :], (128, 128)).T
        code_ref[128 * r : 128 * r + 128, :] = jnp.where((ident & 1) == side, ident >> 1, -1)


def mask_code(ident):
    m = ident.shape[0]
    return pl.pallas_call(
        code_kernel,
        in_specs=[VMEM],
        out_specs=VMEM,
        out_shape=jax.ShapeDtypeStruct((m, 128), jnp.int32),
        compiler_params=params(2),
        cost_estimate=cost(1 << 20, 1 << 20),
        name="mask_code",
    )(ident.reshape(m // 128, 128))


def fetch_kernel(x_ref, here_ref, half_ref, sems):
    width, rows = here_ref.shape[1], half_ref.shape[0]
    at = pl.multiple_of(lax.axis_index("tp") * width, width)
    here = pltpu.make_async_copy(x_ref.at[:, pl.ds(at, width)], here_ref, sems.at[0])
    half = pltpu.make_async_copy(x_ref.at[pl.ds(0, rows)], half_ref, sems.at[1])
    here.start()
    half.start()
    here.wait()
    half.wait()


def fetch(x, width):
    m, k = x.shape
    return pl.pallas_call(
        fetch_kernel,
        in_specs=[HBM],
        out_specs=[VMEM] * 2,
        out_shape=[jax.ShapeDtypeStruct((m, width), BF), jax.ShapeDtypeStruct((m // 2, k), BF)],
        scratch_shapes=[pltpu.SemaphoreType.DMA((2,))],
        compiler_params=params(28),
        cost_estimate=cost(1000000, 1 << 20),
        name="fetch",
    )(x)


def multiply(x_ref, w_ref, o_ref, rows, at=0, block=256):
    def step(i, _):
        here = pl.ds(pl.multiple_of(i * block, block), block)
        there = pl.ds(pl.multiple_of(at + i * block, block), block)
        o_ref[there, :] = jnp.dot(x_ref[here, :], w_ref[...], preferred_element_type=F32)
        return 0

    lax.fori_loop(0, rows // block, step, 0)


def base_kernel(half_ref, w_ref, x_ref, o_ref, rest_ref, xb, sems):
    half, most, last = half_ref.shape[0], o_ref.shape[0], rest_ref.shape[0]
    copies = [
        pltpu.make_async_copy(x_ref.at[pl.ds(half, most - half)], xb, sems.at[0]),
        pltpu.make_async_copy(x_ref.at[pl.ds(most, last)], rest_ref, sems.at[1]),
    ]
    for copy in copies:
        copy.start()
    multiply(half_ref, w_ref, o_ref, half)
    copies[0].wait()
    multiply(xb, w_ref, o_ref, most - half, half)
    copies[1].wait()


def base_first(half, w, x):
    (m, k), n = x.shape, w.shape[1]
    return pl.pallas_call(
        base_kernel,
        in_specs=[VMEM, VMEM, HBM],
        out_specs=[VMEM, VMEM],
        out_shape=[jax.ShapeDtypeStruct((m * 3 // 4, n), F32), jax.ShapeDtypeStruct((m // 4, k), BF)],
        scratch_shapes=[pltpu.VMEM((m // 4, k), BF), pltpu.SemaphoreType.DMA((2,))],
        compiler_params=params(28),
        cost_estimate=cost(5000000000, 1 << 20),
        name="base_first",
    )(half, w, x)


def base_second_kernel(x_ref, w_ref, o_ref):
    multiply(x_ref, w_ref, o_ref, x_ref.shape[0])


def base_second(rest, w):
    return pl.pallas_call(
        base_second_kernel,
        in_specs=[VMEM, VMEM],
        out_specs=VMEM,
        out_shape=jax.ShapeDtypeStruct((rest.shape[0], w.shape[1]), F32),
        compiler_params=params(12),
        cost_estimate=cost(5000000000, 1 << 20),
        name="base_second",
    )(rest, w)


def shrink_kernel(groups, has_sum, last, code_ref, x_ref, *refs):
    code = code_ref[...]
    refs = list(refs)
    total = None
    for count, places in groups:
        parts = [refs.pop(0)[...] for _ in range(count)]
        a = parts[0] if count == 1 else jnp.concatenate(parts, axis=0)
        p = lax.dot_general(x_ref[...], a, (((1,), (1,)), ((), ())), preferred_element_type=F32)
        for k, (j, i) in enumerate(places):
            term = jnp.where(code == owner(j, i), p[:, 128 * k : 128 * k + 128], 0.0)
            total = term if total is None else total + term
    if has_sum:
        total = total + refs.pop(0)[...]
    if not last:
        refs[0][...] = total
        return
    keep_ref, give_ref = refs
    half = total.shape[0] // 2
    folded = total + pltpu.roll(total, 64, 1)
    lane = lax.broadcasted_iota(jnp.int32, (half, 128), 1)
    packed = jnp.where(lane < 64, folded[:half], folded[half:])
    low, high = packed[: half // 2], packed[half // 2 :]
    core = lax.axis_index("tp") % 2
    keep_ref[...] = jnp.where(core == 0, low, high)
    give_ref[...] = jnp.where(core == 0, high, low)


def shrink(code, x, groups, total, last, name, weight=1 << 20):
    m = x.shape[0]
    args = [code, x] + [a for parts, _ in groups for a in parts] + ([] if total is None else [total])
    rows = m // 4 if last else m
    shape = jax.ShapeDtypeStruct((rows, 128), F32)
    return pl.pallas_call(
        functools.partial(
            shrink_kernel, [(len(parts), places) for parts, places in groups], total is not None, last
        ),
        in_specs=[VMEM] * len(args),
        out_specs=[VMEM] * 2 if last else VMEM,
        out_shape=[shape] * 2 if last else shape,
        compiler_params=params(16),
        cost_estimate=cost(weight, 1 << 20),
        name=name,
    )(*args)


UP_PLACES = [[(i, 64 * j, 64)] for i in range(3) for j in range(3)]
UP_PLACES.insert(3, [(5, 0, 64)])
UP_PLACES.insert(7, [(3, 96, 64)])
UP_PLACES.insert(11, [(4, 96, 64)])
UP_PLACES += [[(3, 0, 64)], [(3, 64, 32), (4, 0, 32)], [(4, 32, 64)], [(6, 0, 64)]]


def expand_kernel(code_ref, mine_ref, other_ref, top_ref, bottom_ref, *refs):
    *b_refs, o_ref, b_all = refs
    block = o_ref.shape[0]
    step = pl.program_id(0)
    here = pl.ds(pl.multiple_of(step * block, block), block)
    code = code_ref[here, :]
    core = lax.axis_index("tp") % 2
    mine, other = mine_ref[...].astype(F32), other_ref[...].astype(F32)
    packed = jnp.concatenate(
        [jnp.where(core == 0, mine, other), jnp.where(core == 0, other, mine)], axis=0
    )
    lane = lax.broadcasted_iota(jnp.int32, packed.shape, 1)
    left = (lane < 64) == (step == 0)
    rows = jnp.where(left, packed, pltpu.roll(packed, 64, 1))
    n = o_ref.shape[1]

    @pl.when(step == 0)
    def _():
        for k, pieces in enumerate(UP_PLACES):
            to = 128 * k
            for side in range(2):
                for part, at, count in pieces:
                    b_all[pl.ds(to, count), :] = b_refs[part][pl.ds(at, count), n * side : n * side + n]
                    to += count

    spread = jnp.concatenate(
        [jnp.where(code == owner(j, i), rows, 0.0).astype(BF) for i in HOPS for j in HOPS], axis=1
    )
    delta = jnp.dot(spread, b_all[...], preferred_element_type=F32)
    delta = delta.astype(BF).astype(F32)
    quarter = block // 2

    @pl.when(step == 0)
    def _():
        o_ref[...] = (top_ref[:block, :] + adapter_scale * delta).astype(BF)

    @pl.when(step == 1)
    def _():
        o_ref[:quarter, :] = (top_ref[block:, :] + adapter_scale * delta[:quarter]).astype(BF)
        o_ref[quarter:, :] = (bottom_ref[...] + adapter_scale * delta[quarter:]).astype(BF)


def expand(code, mine, other, base, ups):
    m, n = code.shape[0], base[0].shape[1]
    block = m // 2
    args = [code, mine, other, *base, *ups]
    return pl.pallas_call(
        expand_kernel,
        grid=(2,),
        in_specs=[VMEM] * len(args),
        out_specs=pl.BlockSpec((block, n), lambda i: (i, 0)),
        out_shape=jax.ShapeDtypeStruct((m, n), BF),
        scratch_shapes=[pltpu.VMEM((2048, n), BF)],
        compiler_params=params(14),
        cost_estimate=cost(2 * m * n * 2048, 6 * m * n),
        name="expand",
    )(*args)


def tie(*arrays):
    return lax.optimization_barrier(arrays)


def per_device(activations, token_adapter_index, query_matrix, down, up):
    down = jnp.swapaxes(down, 1, 2).reshape(128, -1)
    up = up.reshape(128, -1)
    width = down.shape[1]
    row = lambda j, hops=HOPS: [(j, i) for i in hops]

    near = [first(down, d) for d in (1, -1, 2)]
    code = mask_code(token_adapter_index)
    here, half = fetch(tie(activations, code)[0], width)
    before, after, far, here, half = tie(*near, here, half)
    own_up = jnp.concatenate([up[:64], up[64:]], axis=1)
    top = jnp.concatenate([down, before, own_up], axis=0)
    bottom = jnp.concatenate([after, far, own_up], axis=0)
    top_before, bottom_after = second(top, 1), second(bottom, -1)
    bottom_before, top_after = second(bottom[:256], 1), second(top[:256], -1)
    base, rest = base_first(half, query_matrix, activations)
    top_before, bottom_after, base = tie(top_before, bottom_after, base)

    top_two, bottom_two = second(top_before, 1), second(bottom_after[:256], -1)
    groups = [
        ([top[:256], bottom[:256]], row(0)),
        ([top_before[:256], bottom_before], row(-1)),
        ([top_after, bottom_after[:256]], row(1)),
    ]
    total = shrink(code, here, groups, None, False, "shrink_near", 5000000000)
    column = jnp.concatenate([own_up, top_before[256:], bottom_after[256:]], axis=0)
    column, total = tie(column, total)
    c_before, c_after = first(column, 1), first(column, -1)
    top_two, bottom_two, total = tie(top_two, bottom_two, total)
    d_two = [top_two[:256], bottom_two]
    keep, give = shrink(code, here, [(d_two, row(2))], total, True, "shrink_far")
    keep = keep + other_core(give)
    up_two = top_two[256:]
    w_before = first(jnp.concatenate([c_before[:96], up_two], axis=0), 1)
    w_after = first(jnp.concatenate([c_after[96:], up_two], axis=0), -1)
    w_two = first(up_two, 2)
    keep = keep + pair(keep, 0)
    there, last = tie(pair(keep, 1), base_second(rest, query_matrix))
    mine, *far_ups = tie((keep + there).astype(BF), w_before, w_after, up_two, w_two)
    return expand(code, mine, other_core(mine), [base, last], [column, c_before, c_after, *far_ups])


def solution(mesh):
    in_specs = (
        P("rep", None),
        P("rep", None),
        P(None, "tp"),
        P("rep", "tp", None),
        P("rep", None, "tp"),
    )
    return jax.shard_map(
        per_device, mesh=mesh, in_specs=in_specs, out_specs=P("rep", "tp"), check_vma=False
    )
```

```python
import functools

import jax
import jax.numpy as jnp
from jax import lax
from jax.experimental import pallas as pl
from jax.experimental.pallas import tpu as pltpu
from jax.sharding import PartitionSpec as P

BF, F32 = jnp.bfloat16, jnp.float32
AXES = ("rep", "tp")
RING = 4
HOPS = (0, -1, 1, 2)
adapter_scale = 0.5


def device_of(x, y, z, c):
    return (z % RING * RING + x % RING) * 2 * RING + y % RING * 2 + c


def every(f):
    return [
        (device_of(x, y, z, c), device_of(*f(x, y, z, c)))
        for z in range(RING)
        for x in range(RING)
        for y in range(RING)
        for c in range(2)
    ]


def first(a, d):
    return lax.ppermute(
        a, AXES, every(lambda x, y, z, c: (x, y, z + d, c) if c else (x + d, y, z, c))
    )


def second(a, d):
    return lax.ppermute(
        a, AXES, every(lambda x, y, z, c: (x + d, y, z, c) if c else (x, y, z + d, c))
    )


def other_core(a):
    return lax.ppermute(a, AXES, every(lambda x, y, z, c: (x, y, z, 1 - c)))


def pair(a, step):
    def to(x, y, z, c):
        return (x, (y ^ 1) if (c + step) % 2 == 0 else (3 - y), z, c)

    return lax.ppermute(a, AXES, every(to))


def params(mib):
    return pltpu.CompilerParams(vmem_limit_bytes=mib << 20)


def cost(flops, moved):
    return pl.CostEstimate(flops=flops, bytes_accessed=moved, transcendentals=0)


VMEM = pl.BlockSpec(memory_space=pltpu.VMEM)
HBM = pl.BlockSpec(memory_space=pltpu.HBM)


def owner(j, i):
    rep, core = lax.axis_index("rep"), lax.axis_index("tp") % 2
    dz, dx = jnp.where(core == 0, j, i), jnp.where(core == 0, i, j)
    return (rep // RING + dz + RING) % RING * RING + (rep % RING + dx + RING) % RING


def code_kernel(ident_ref, code_ref):
    side = lax.broadcasted_iota(jnp.int32, (128, 128), 1) // 64
    for r in range(ident_ref.shape[0]):
        ident = jnp.broadcast_to(ident_ref[r : r + 1, :], (128, 128)).T
        code_ref[128 * r : 128 * r + 128, :] = jnp.where((ident & 1) == side, ident >> 1, -1)


def mask_code(ident):
    m = ident.shape[0]
    return pl.pallas_call(
        code_kernel,
        in_specs=[VMEM],
        out_specs=VMEM,
        out_shape=jax.ShapeDtypeStruct((m, 128), jnp.int32),
        compiler_params=params(2),
        cost_estimate=cost(1 << 20, 1 << 20),
        name="mask_code",
    )(ident.reshape(m // 128, 128))


def fetch_kernel(x_ref, here_ref, half_ref, sems):
    width, rows = here_ref.shape[1], half_ref.shape[0]
    at = pl.multiple_of(lax.axis_index("tp") * width, width)
    here = pltpu.make_async_copy(x_ref.at[:, pl.ds(at, width)], here_ref, sems.at[0])
    half = pltpu.make_async_copy(x_ref.at[pl.ds(0, rows)], half_ref, sems.at[1])
    here.start()
    half.start()
    here.wait()
    half.wait()


def fetch(x, width):
    m, k = x.shape
    return pl.pallas_call(
        fetch_kernel,
        in_specs=[HBM],
        out_specs=[VMEM] * 2,
        out_shape=[jax.ShapeDtypeStruct((m, width), BF), jax.ShapeDtypeStruct((m // 2, k), BF)],
        scratch_shapes=[pltpu.SemaphoreType.DMA((2,))],
        compiler_params=params(28),
        cost_estimate=cost(1000000, 1 << 20),
        name="fetch",
    )(x)


def multiply(x_ref, w_ref, o_ref, rows, at=0, block=256):
    def step(i, _):
        here = pl.ds(pl.multiple_of(i * block, block), block)
        there = pl.ds(pl.multiple_of(at + i * block, block), block)
        o_ref[there, :] = jnp.dot(x_ref[here, :], w_ref[...], preferred_element_type=F32)
        return 0

    lax.fori_loop(0, rows // block, step, 0)


def base_kernel(half_ref, w_ref, x_ref, o_ref, rest_ref, xb, sems):
    half, most, last = half_ref.shape[0], o_ref.shape[0], rest_ref.shape[0]
    copies = [
        pltpu.make_async_copy(x_ref.at[pl.ds(half, most - half)], xb, sems.at[0]),
        pltpu.make_async_copy(x_ref.at[pl.ds(most, last)], rest_ref, sems.at[1]),
    ]
    for copy in copies:
        copy.start()
    multiply(half_ref, w_ref, o_ref, half)
    copies[0].wait()
    multiply(xb, w_ref, o_ref, most - half, half)
    copies[1].wait()


def base_first(half, w, x):
    (m, k), n = x.shape, w.shape[1]
    return pl.pallas_call(
        base_kernel,
        in_specs=[VMEM, VMEM, HBM],
        out_specs=[VMEM, VMEM],
        out_shape=[jax.ShapeDtypeStruct((m * 3 // 4, n), F32), jax.ShapeDtypeStruct((m // 4, k), BF)],
        scratch_shapes=[pltpu.VMEM((m // 4, k), BF), pltpu.SemaphoreType.DMA((2,))],
        compiler_params=params(28),
        cost_estimate=cost(5000000000, 1 << 20),
        name="base_first",
    )(half, w, x)


def base_second_kernel(x_ref, w_ref, o_ref):
    multiply(x_ref, w_ref, o_ref, x_ref.shape[0])


def base_second(rest, w):
    return pl.pallas_call(
        base_second_kernel,
        in_specs=[VMEM, VMEM],
        out_specs=VMEM,
        out_shape=jax.ShapeDtypeStruct((rest.shape[0], w.shape[1]), F32),
        compiler_params=params(12),
        cost_estimate=cost(5000000000, 1 << 20),
        name="base_second",
    )(rest, w)


def shrink_kernel(groups, has_sum, last, code_ref, x_ref, *refs):
    code = code_ref[...]
    refs = list(refs)
    total = None
    for count, places in groups:
        parts = [refs.pop(0)[...] for _ in range(count)]
        a = parts[0] if count == 1 else jnp.concatenate(parts, axis=0)
        p = lax.dot_general(x_ref[...], a, (((1,), (1,)), ((), ())), preferred_element_type=F32)
        for k, (j, i) in enumerate(places):
            term = jnp.where(code == owner(j, i), p[:, 128 * k : 128 * k + 128], 0.0)
            total = term if total is None else total + term
    if has_sum:
        total = total + refs.pop(0)[...]
    if not last:
        refs[0][...] = total
        return
    keep_ref, give_ref = refs
    half = total.shape[0] // 2
    folded = total + pltpu.roll(total, 64, 1)
    lane = lax.broadcasted_iota(jnp.int32, (half, 128), 1)
    packed = jnp.where(lane < 64, folded[:half], folded[half:])
    low, high = packed[: half // 2], packed[half // 2 :]
    core = lax.axis_index("tp") % 2
    keep_ref[...] = jnp.where(core == 0, low, high)
    give_ref[...] = jnp.where(core == 0, high, low)


def shrink(code, x, groups, total, last, name, weight=1 << 20):
    m = x.shape[0]
    args = [code, x] + [a for parts, _ in groups for a in parts] + ([] if total is None else [total])
    rows = m // 4 if last else m
    shape = jax.ShapeDtypeStruct((rows, 128), F32)
    return pl.pallas_call(
        functools.partial(
            shrink_kernel, [(len(parts), places) for parts, places in groups], total is not None, last
        ),
        in_specs=[VMEM] * len(args),
        out_specs=[VMEM] * 2 if last else VMEM,
        out_shape=[shape] * 2 if last else shape,
        compiler_params=params(16),
        cost_estimate=cost(weight, 1 << 20),
        name=name,
    )(*args)


def expand_kernel(groups, code_ref, mine_ref, other_ref, top_ref, bottom_ref, *refs):
    b_refs, o_ref = refs[:-1], refs[-1]
    block = o_ref.shape[0]
    step = pl.program_id(0)
    here = pl.ds(pl.multiple_of(step * block, block), block)
    code = code_ref[here, :]
    core = lax.axis_index("tp") % 2
    mine, other = mine_ref[...].astype(F32), other_ref[...].astype(F32)
    packed = jnp.concatenate(
        [jnp.where(core == 0, mine, other), jnp.where(core == 0, other, mine)], axis=0
    )
    lane = lax.broadcasted_iota(jnp.int32, packed.shape, 1)
    left = (lane < 64) == (step == 0)
    rows = jnp.where(left, packed, pltpu.roll(packed, 64, 1))
    delta = None
    for (places, ref_at, lanes), b_ref in zip(groups, b_refs):
        spread = jnp.concatenate(
            [jnp.where(code == owner(j, i), rows, 0.0).astype(BF) for j, i in places], axis=1
        )
        d = jnp.dot(spread, b_ref[ref_at:, lanes : lanes + o_ref.shape[1]], preferred_element_type=F32)
        delta = d if delta is None else delta + d
    delta = delta.astype(BF).astype(F32)
    quarter = block // 2

    @pl.when(step == 0)
    def _():
        o_ref[...] = (top_ref[:block, :] + adapter_scale * delta).astype(BF)

    @pl.when(step == 1)
    def _():
        o_ref[:quarter, :] = (top_ref[block:, :] + adapter_scale * delta[:quarter]).astype(BF)
        o_ref[quarter:, :] = (bottom_ref[...] + adapter_scale * delta[quarter:]).astype(BF)


def expand(code, mine, other, base, parts):
    m, n = code.shape[0], base[0].shape[1]
    block = m // 2
    args = [code, mine, other, *base] + [part[0] for part in parts]
    return pl.pallas_call(
        functools.partial(expand_kernel, [part[1:] for part in parts]),
        grid=(2,),
        in_specs=[VMEM] * len(args),
        out_specs=pl.BlockSpec((block, n), lambda i: (i, 0)),
        out_shape=jax.ShapeDtypeStruct((m, n), BF),
        compiler_params=params(12),
        cost_estimate=cost(2 * m * n * 2048, 6 * m * n),
        name="expand",
    )(*args)


def tie(*arrays):
    return lax.optimization_barrier(arrays)


def per_device(activations, token_adapter_index, query_matrix, down, up):
    down = jnp.swapaxes(down, 1, 2).reshape(128, -1)
    up = up.reshape(128, -1)
    width = down.shape[1]
    row = lambda j, hops=HOPS: [(j, i) for i in hops]

    near = [first(down, d) for d in (1, -1, 2)]
    code = mask_code(token_adapter_index)
    here, half = fetch(tie(activations, code)[0], width)
    before, after, far, here, half = tie(*near, here, half)
    top, bottom = jnp.concatenate([down, before], axis=0), jnp.concatenate([after, far], axis=0)
    top_before, bottom_after = second(top, 1), second(bottom, -1)
    bottom_before, top_after = second(bottom, 1), second(top, -1)
    base, rest = base_first(half, query_matrix, activations)
    top_before, bottom_after, base, up = tie(top_before, bottom_after, base, up)

    d_two = [second(top_before, 1), second(bottom_after, -1)]
    u_own = jnp.concatenate([up] + [first(up, d) for d in (1, -1, 2)], axis=0)
    groups = [([top, bottom], row(0)), ([top_before, bottom_before], row(-1)), ([top_after, bottom_after], row(1))]
    total = shrink(code, here, groups, None, False, "shrink_near", 5000000000)
    total, u_own = tie(total, u_own)
    u_before, u_after = second(u_own, 1), second(u_own, -1)
    *d_two, total = tie(*d_two, total)
    keep, give = shrink(code, here, [(d_two, row(2))], total, True, "shrink_far")
    keep = keep + other_core(give)
    u_two = [second(u_before[:256], 1), second(u_after[256:], -1)]
    keep = keep + pair(keep, 0)
    there, last, *u_two = tie(pair(keep, 1), base_second(rest, query_matrix), *u_two)
    keep = keep + there
    mine = keep.astype(BF)
    parts = [(u_own, row(0), 0, 0), (u_before, row(-1), 0, 0), (u_after, row(1), 0, 0)]
    parts += [(a, row(2, hops), 0, 0) for a, hops in zip(u_two, (HOPS[:2], HOPS[2:]))]
    return expand(code, mine, other_core(mine), [base, last], parts)


def solution(mesh):
    in_specs = (
        P("rep", None),
        P("rep", None),
        P(None, "tp"),
        P("rep", "tp", None),
        P("rep", None, "tp"),
    )
    return jax.shard_map(
        per_device, mesh=mesh, in_specs=in_specs, out_specs=P("rep", "tp"), check_vma=False
    )
```
